32 devices in a mesh: ens: 2 (over y), tile: 4 (over z), trc: 2 (over x), lev: 2 (over core).
Axes of the slice: x: 2, y: 2, z: 4, core: 2. Of those that a mesh axis runs over, the one named last changes fastest.
Arguments:
- tracers: float32 [32, 16, 64, 128], P('trc', 'lev', ('ens', 'tile')), parts along dimension 2, may hold values from -6 to 6
- cotangent: float32 [32, 16, 64, 128], P('trc', 'lev', ('ens', 'tile')), parts along dimension 2, may hold values from -3 to 3
- zonal_speed: float32 [16, 64, 128], P('lev', ('ens', 'tile')), parts along dimension 1, may hold values from -0.3 to 0.3
- meridional_speed: float32 [16, 64, 128], P('lev', ('ens', 'tile')), parts along dimension 1, may hold values from -0.3 to 0.3
- vertical_speed: float32 [16, 64, 128], P('lev', ('ens', 'tile')), parts along dimension 1, may hold values from -0.3 to 0.3
- lateral_mixing: float32 [16, 64, 128], P('lev', ('ens', 'tile')), parts along dimension 1, may hold values from 0.01 to 0.08
- vertical_mixing: float32 [16, 64, 128], P('lev', ('ens', 'tile')), parts along dimension 1, may hold values from 0.02 to 0.16
- column_depth: int32 [64, 128], P(('ens', 'tile')), parts along dimension 0, may hold values from 0 to 16
Outputs:
- start_cotangent: float32 [32, 16, 64, 128], P('trc', 'lev', ('ens', 'tile')), parts along dimension 2
- speed_cotangent: float32 [3, 16, 64, 128], P(None, ('lev', 'trc'), ('ens', 'tile')), parts along dimension 2
The draws below stay inside these ranges and needn't reach their ends.
There are 2 independent parts, one for each index of `ens`. The reference program is written for one: setup_inputs(seed, part) draws one part's arguments, and reference() takes and returns one part's arrays. A program takes and returns all parts, laid end to end along the dimension named above; each array names one. Nothing has to cross between parts.
All inputs are finite; a program needn't handle non-finite values.
Results may differ from the reference program's by a relative error of at most 0.0003.
Values sent between devices are 32-bit elements; how exact they have to be, the bound alone decides.
A program may use at most 64 MiB of HBM per device.

```python
import math
import jax
import jax.numpy as jnp
from jax import lax

LEVELS = 16
TRACERS = 32
NX = 32
NY = 128


def place_ends(values, own_key, smallest, largest):
    longest = values.shape.index(max(values.shape))
    spots = []
    for shift in (0, 1):
        where = [jax.random.randint(jax.random.fold_in(own_key, axis), (), 0, length) for axis, length in enumerate(values.shape)]
        where[longest] = (where[longest] + shift) % values.shape[longest]
        spots.append(tuple(where))
    return values.at[spots[0]].set(smallest).at[spots[1]].set(largest)


def block_scale(key, shape, shards, low, top_value):
    def one(position, blocks):
        draws = jax.random.uniform(jax.random.fold_in(jax.random.fold_in(key, 6), position), (blocks,), jnp.float32, low / len(shards), top_value / len(shards))
        return jnp.repeat(jnp.exp(draws), shape[position] // blocks).reshape((-1,) + (1,) * (len(shape) - position - 1))

    level = one(*shards[0])
    for cut in shards[1:]:
        level = level * one(*cut)
    return level


def noise(stream_key, dims, scale, most, split=(), held_as=jnp.bfloat16):
    gain = block_scale(stream_key, dims, split, -0.22, 0.18) if split else 1.0
    array = jax.random.normal(stream_key, dims, jnp.float32) * scale * gain
    return jnp.minimum(jnp.maximum(array, -most), most).astype(held_as)


def setup_inputs(seed: int = 0, part: int = 0) -> dict:
    streams_of = jax.random.split(jax.random.key(seed), 9)
    part_splits = jax.random.split(jax.random.fold_in(streams_of[8], part), 9)
    tracers = noise(part_splits[0], (TRACERS, LEVELS, NX, NY), 1.0, 6.0, ((0, 2), (1, 2), (2, 4)), jnp.float32)
    cotangent = noise(part_splits[1], (TRACERS, LEVELS, NX, NY), 0.5, 3.0, ((0, 2), (1, 2), (2, 4)), jnp.float32)
    zonal_speed = noise(part_splits[2], (LEVELS, NX, NY), 0.1, 0.3, ((0, 2), (1, 4)), jnp.float32)
    meridional_speed = noise(part_splits[3], (LEVELS, NX, NY), 0.1, 0.3, ((0, 2), (1, 4)), jnp.float32)
    vertical_speed = noise(part_splits[4], (LEVELS, NX, NY), 0.1, 0.3, ((0, 2), (1, 4)), jnp.float32)
    lateral_mixing = jnp.clip(jnp.exp(math.log(0.08) - 2.0794415 * jax.random.uniform(part_splits[5], (LEVELS, NX, NY), jnp.float32) ** block_scale(part_splits[5], (LEVELS, NX, NY), ((0, 2), (1, 4)), -0.2, 0.2)), 0.01, 0.08)
    vertical_mixing = jnp.clip(jnp.exp(math.log(0.16) - 2.0794415 * jax.random.uniform(part_splits[6], (LEVELS, NX, NY), jnp.float32) ** block_scale(part_splits[6], (LEVELS, NX, NY), ((0, 2), (1, 4)), -0.2, 0.2)), 0.02, 0.16)
    column_depth = place_ends(jax.random.randint(part_splits[7], (NX, NY), 0, LEVELS + 1), jax.random.fold_in(part_splits[7], 1), 0, LEVELS).astype(jnp.int32)
    return {"tracers": tracers, "cotangent": cotangent, "zonal_speed": zonal_speed, "meridional_speed": meridional_speed, "vertical_speed": vertical_speed, "lateral_mixing": lateral_mixing, "vertical_mixing": vertical_mixing, "column_depth": column_depth}


albada_floor = 0.01

def albada(lower_step, upper_step):
    return lower_step * upper_step * (lower_step + upper_step) / (lower_step * lower_step + upper_step * upper_step + albada_floor)

def face_flux(far_behind, behind, beyond, far_beyond, velocity, spread, opened):
    rising = behind + 0.5 * albada(behind - far_behind, beyond - behind)
    falling = beyond - 0.5 * albada(beyond - behind, far_beyond - beyond)
    carried = jnp.where(velocity >= 0.0, rising, falling)
    return opened * (velocity * carried - spread * (beyond - behind))

def window(values, direction, offset):
    leading = values.ndim - 3
    pieces = [slice(None)] * leading
    for spatial in range(3):
        extent = values.shape[leading + spatial] - 4
        if spatial == direction:
            pieces.append(slice(offset, extent + 1 + offset))
        else:
            pieces.append(slice(2, extent + 2))
    return values[tuple(pieces)]

def advance(padded, fields):
    wetness = fields[5]
    result = padded[:, 2:-2, 2:-2, 2:-2]
    for direction, speed_row, spread_row in ((0, 2, 4), (1, 0, 3), (2, 1, 3)):
        through = face_flux(window(padded, direction, 0), window(padded, direction, 1), window(padded, direction, 2), window(padded, direction, 3), window(fields[speed_row], direction, 2), window(fields[spread_row], direction, 2), window(wetness, direction, 1) * window(wetness, direction, 2))
        extent = through.shape[direction + 1]
        result = result + lax.slice_in_dim(through, 0, extent - 1, axis=direction + 1) - lax.slice_in_dim(through, 1, extent, axis=direction + 1)
    return result

def reference(tracers, cotangent, zonal_speed, meridional_speed, vertical_speed, lateral_mixing, vertical_mixing, column_depth):
    levels = tracers.shape[1]
    wetness = (jnp.arange(levels, dtype=jnp.int32)[:, None, None] < column_depth[None]).astype(jnp.float32)
    others = jnp.stack([lateral_mixing, vertical_mixing, wetness])
    speeds = jnp.stack([zonal_speed, meridional_speed, vertical_speed])

    def single(tracer_field, speed_set):
        padded = jnp.pad(tracer_field[None], ((0, 0), (2, 2), (2, 2), (2, 2)))
        fields = jnp.pad(jnp.concatenate([speed_set, others]), ((0, 0), (2, 2), (2, 2), (2, 2)))
        return advance(padded, fields)[0]

    def per_tracer(summed, slices):
        initial, final_cot = slices
        middle = single(initial, speeds)
        _, pull_late = jax.vjp(single, middle, speeds)
        middle_cot, late_speed = pull_late(final_cot)
        _, pull_early = jax.vjp(single, initial, speeds)
        start_cot, early_speed = pull_early(middle_cot)
        return (summed + late_speed + early_speed, start_cot)
    summed, start_cotangent = lax.scan(per_tracer, jnp.zeros_like(speeds), (tracers, cotangent))
    return (start_cotangent, summed)
```

```python
import functools

import jax
import jax.numpy as jnp
from jax import lax
from jax.experimental import pallas as pl
from jax.experimental.pallas import tpu as pltpu
from jax.sharding import PartitionSpec as P

ALBADA_FLOOR = 0.01
MESH = pl.DeviceIdType.MESH
ROWS = 8


def inverse(values):
    return pl.reciprocal(values, approx=True)


def limiter(lower, upper, lower_square, upper_square):
    half_inverse = inverse(lower_square + upper_square)
    product = lower * upper
    total = lower + upper
    return product * total * half_inverse, half_inverse, total


def doubled_square(step):
    return step * (step + step) + ALBADA_FLOOR


def forward_line(count, q, rise, fall, spread, emit):
    values = {x: q(x) for x in range(-2, count + 2)}
    steps = {c: values[c] - values[c - 1] for c in range(-1, count + 2)}
    squares = {c: doubled_square(steps[c]) for c in steps}
    through = {}
    above = None
    for x in range(-1, count + 1):
        slope, _, _ = limiter(steps[x], steps[x + 1], squares[x], squares[x + 1])
        if x >= 0:
            through[x] = (
                rise(x) * above + fall(x) * (values[x] - slope) - spread(x) * steps[x]
            )
        above = values[x] + slope
        if x >= 1:
            emit(x - 1, through[x - 1] - through[x])


def backward_line(count, q, g, rise, fall, spread, emit, speed):
    values = {x: q(x) for x in range(-2, count + 2)}
    steps = {c: values[c] - values[c - 1] for c in range(-1, count + 2)}
    squares = {c: doubled_square(steps[c]) for c in steps}
    cots = {x: g(x) for x in range(-2, count + 2)}
    up, down, jump, falls = {}, {}, {}, {}
    faces = {c: cots[c] - cots[c - 1] for c in range(-1, count + 2)}
    for c in range(0, count + 2):
        up[c] = faces[c] * rise(c)
    for c in range(-1, count + 1):
        falls[c] = fall(c)
        down[c] = faces[c] * falls[c]
    above, later = None, None
    for x in range(-1, count + 1):
        lower, upper = steps[x], steps[x + 1]
        slope, half_inverse, total = limiter(lower, upper, squares[x], squares[x + 1])
        weight = half_inverse * (up[x + 1] - down[x])
        fourfold = 4.0 * slope
        if x >= 0:
            first = (upper * (lower + total) - lower * fourfold) * weight
            jump[x] = first + later - spread(x) * faces[x]
        if x < count:
            later = (lower * (upper + total) - upper * fourfold) * weight
        if 0 <= x < count:
            carried = jnp.where(falls[x] < 0.0, values[x] - slope, above)
            speed(x, faces[x] * carried)
        above = values[x] + slope
        if x >= 1:
            emit(x - 1, (jump[x - 1] - jump[x]) + (up[x] + down[x - 1]))


def across(values, lane, last):
    before = jnp.where(lane == 0, 0.0, pltpu.roll(values, 1, 1))
    lower = values - before
    upper = jnp.where(lane == last, -values, pltpu.roll(lower, last, 1))
    return lower, upper


def forward_cell(values, rise, fall, spread, lane, last):
    lower, upper = across(values, lane, last)
    slope, _, _ = limiter(lower, upper, doubled_square(lower), doubled_square(upper))
    above = pltpu.roll(values + slope, 1, 1)
    through = rise * above + fall * (values - slope) - spread * lower
    return through - pltpu.roll(through, last, 1)


def backward_cell(values, cot, rise, fall, spread, lane, last):
    lower, upper = across(values, lane, last)
    slope, half_inverse, total = limiter(
        lower, upper, doubled_square(lower), doubled_square(upper)
    )
    face = cot - pltpu.roll(cot, 1, 1)
    up = pltpu.roll(face * rise, last, 1)
    down = face * fall
    weight = half_inverse * (up - down)
    fourfold = 4.0 * slope
    first = (upper * (lower + total) - lower * fourfold) * weight
    later = (lower * (upper + total) - upper * fourfold) * weight
    near = first - spread * face
    result = (
        near
        - later
        + up
        + down
        + jnp.where(lane == 0, 0.0, pltpu.roll(later, 1, 1))
        - jnp.where(lane == last, 0.0, pltpu.roll(near, last, 1))
    )
    carried = jnp.where(fall < 0.0, values - slope, pltpu.roll(values + slope, 1, 1))
    return result, face * carried


def kernel(
    sizes,
    dims,
    tracer_ref,
    cot_ref,
    zonal_ref,
    merid_ref,
    vert_ref,
    lateral_ref,
    vmix_ref,
    depth_ref,
    start_ref,
    speed_ref,
    first,
    last_cot,
    middle,
    middle_cot,
    pack,
    packed,
    vert_ext,
    vmix_ext,
    zonal_fields,
    vert_fields,
    merid_fields,
    opened_all,
    sums,
    reduced,
    arrived,
    halo_send,
    halo_recv,
    field_send,
    field_recv,
    sum_send,
    sum_recv,
):
    tiles, levs, groups_trc = sizes
    tracers, levels, columns, lanes = dims
    groups = tracers // ROWS
    end = lanes - 1
    cells = levels * columns
    tile, lev, trc = lax.axis_index("tile"), lax.axis_index("lev"), lax.axis_index("trc")
    lane = lax.broadcasted_iota(jnp.int32, (ROWS, lanes), 1)

    below = {"tile": tile > 0, "lev": lev > 0}
    beyond = {"tile": tile < tiles - 1, "lev": lev < levs - 1}
    place = {"tile": tile, "lev": lev}
    size = {"tile": tiles, "lev": levs}
    axes = [axis for axis in ("tile", "lev") if size[axis] > 1]

    barrier = pltpu.get_barrier_semaphore()
    expected = groups_trc - 1
    for axis in axes:
        for there, offset in ((below[axis], -1), (beyond[axis], 1)):

            @pl.when(there)
            def _(axis=axis, offset=offset):
                pl.semaphore_signal(
                    barrier,
                    inc=1,
                    device_id={axis: place[axis] + offset},
                    device_id_type=MESH,
                )

            expected = expected + there.astype(jnp.int32)
    for step in range(1, groups_trc):
        pl.semaphore_signal(
            barrier,
            inc=1,
            device_id={"trc": lax.rem(trc + step, groups_trc)},
            device_id_type=MESH,
        )

    def wet(level):
        known = jnp.logical_and(level < depth_ref[...], level >= 0)
        return jnp.where(known, 1.0, 0.0)

    def load_own(l, carry):
        for g in range(groups):
            for i in range(columns):
                rows = pl.ds(g * ROWS * cells + l * columns + i, ROWS, stride=cells)
                first[g, l + 2, i + 2] = tracer_ref[rows, :]
                last_cot[g, l + 2, i + 2] = cot_ref[rows, :]
        here = wet(lev * levels + l)
        zonal, lateral = zonal_ref[l], lateral_ref[l]
        for side, rows in ((0, slice(0, 2)), (1, slice(columns - 2, columns))):
            pack[side, l] = jnp.concatenate(
                [zonal[rows], lateral[rows], here[rows], here[rows]], axis=0
            )
        vert_ext[l + 2] = vert_ref[l]
        vmix_ext[l + 2] = vmix_ref[l]
        return carry

    lax.fori_loop(0, levels, load_own, 0)

    zero_tile = jnp.zeros((ROWS, lanes), jnp.float32)

    def clear(side):
        for buffer in (first, last_cot, middle, middle_cot):
            for g in range(groups):
                if side < 2:
                    place_at = columns + 2 if side == 0 else 0

                    def clear_row(l, carry):
                        buffer[g, l + 2, place_at] = zero_tile
                        buffer[g, l + 2, place_at + 1] = zero_tile
                        return carry

                    lax.fori_loop(0, levels, clear_row, 0)
                else:
                    place_at = levels + 2 if side == 2 else 0

                    def clear_column(i, carry):
                        buffer[g, place_at, i + 2] = zero_tile
                        buffer[g, place_at + 1, i + 2] = zero_tile
                        return carry

                    lax.fori_loop(0, columns, clear_column, 0)
        if side < 2:
            packed[side] = jnp.zeros_like(packed[side])
        else:
            place_at = levels + 2 if side == 2 else 0
            for buffer in (vert_ext, vmix_ext):
                buffer[place_at] = zero_tile_rows
                buffer[place_at + 1] = zero_tile_rows

    zero_tile_rows = jnp.zeros((columns, lanes), jnp.float32)
    for side, axis, there in (
        (0, "tile", beyond["tile"]),
        (1, "tile", below["tile"]),
        (2, "lev", beyond["lev"]),
        (3, "lev", below["lev"]),
    ):
        if size[axis] > 1:

            @pl.when(jnp.logical_not(there))
            def _(side=side):
                clear(side)

        else:
            clear(side)

    pl.semaphore_wait(barrier, expected)

    def exchange(pairs, send_sem, recv_sem):
        copies = []
        for side, source, destination in pairs:
            axis = "tile" if side in (0, 1) else "lev"
            if size[axis] == 1:
                continue
            goes_down = side in (0, 2)
            copy = pltpu.make_async_remote_copy(
                src_ref=source,
                dst_ref=destination,
                send_sem=send_sem(side),
                recv_sem=recv_sem(side),
                device_id={axis: place[axis] + (-1 if goes_down else 1)},
                device_id_type=MESH,
            )
            sends = below[axis] if goes_down else beyond[axis]
            receives = beyond[axis] if goes_down else below[axis]
            copies.append((copy, sends, receives))
        return copies

    def start(copies):
        for copy, sends, _ in copies:
            pl.when(sends)(copy.start)

    def arrive(copies):
        for copy, _, receives in copies:
            pl.when(receives)(copy.wait_recv)

    def finish(copies):
        for copy, sends, _ in copies:
            pl.when(sends)(copy.wait_send)

    own_l, own_i = pl.ds(2, levels), pl.ds(2, columns)

    def halo(buffer, stage, g):
        pairs = [
            (0, buffer.at[g, own_l, pl.ds(2, 2)], buffer.at[g, own_l, pl.ds(columns + 2, 2)]),
            (1, buffer.at[g, own_l, pl.ds(columns, 2)], buffer.at[g, own_l, pl.ds(0, 2)]),
            (2, buffer.at[g, pl.ds(2, 2), own_i], buffer.at[g, pl.ds(levels + 2, 2), own_i]),
            (3, buffer.at[g, pl.ds(levels, 2), own_i], buffer.at[g, pl.ds(0, 2), own_i]),
        ]
        return exchange(
            pairs,
            lambda side: halo_send.at[stage, g, side],
            lambda side: halo_recv.at[stage, g, side],
        )

    field_copies = exchange(
        [(0, pack.at[0], packed.at[0]), (1, pack.at[1], packed.at[1])],
        lambda side: field_send.at[0, side],
        lambda side: field_recv.at[0, side],
    )
    for row, buffer in enumerate((vert_ext, vmix_ext)):
        field_copies += exchange(
            [
                (2, buffer.at[pl.ds(2, 2)], buffer.at[pl.ds(levels + 2, 2)]),
                (3, buffer.at[pl.ds(levels, 2)], buffer.at[pl.ds(0, 2)]),
            ],
            lambda side, row=row: field_send.at[row, side],
            lambda side, row=row: field_recv.at[row, side],
        )
    first_copies = [halo(first, 0, g) for g in range(groups)]
    cot_copies = [halo(last_cot, 1, g) for g in range(groups)]
    middle_copies = [halo(middle, 2, g) for g in range(groups)]
    back_copies = [halo(middle_cot, 3, g) for g in range(groups)]

    start(field_copies)
    for copies in first_copies + cot_copies:
        start(copies)

    def spread_rows(target, head, opened, speed, mixing, count):
        kinds = (
            opened * jnp.maximum(speed, 0.0),
            opened * jnp.minimum(speed, 0.0),
            opened * mixing,
        )
        for kind, values in enumerate(kinds):
            for i in range(count):
                target[(kind,) + head + (i,)] = jnp.broadcast_to(
                    values[i : i + 1], (ROWS, lanes)
                )

    def merid_build(l, carry):
        here = wet(lev * levels + l)
        south = jnp.where(lane[:columns] == 0, 0.0, pltpu.roll(here, 1, 1))
        opened = here * south
        opened_all[1, l] = opened
        spread_rows(merid_fields, (l,), opened, merid_ref[l], lateral_ref[l], columns)
        return carry

    lax.fori_loop(0, levels, merid_build, 0)

    def forward_merid(g):
        def step(l, carry):
            for i in range(columns):
                values = first[g, l + 2, i + 2]
                middle[g, l + 2, i + 2] = values + forward_cell(
                    values,
                    merid_fields[0, l, i],
                    merid_fields[1, l, i],
                    merid_fields[2, l, i],
                    lane,
                    end,
                )
            return carry

        lax.fori_loop(0, levels, step, 0)

    for g in range(groups):
        forward_merid(g)

    arrive(field_copies)

    def zonal_build(l, carry):
        low, high = packed[1, l], packed[0, l]
        here = wet(lev * levels + l)
        wets = jnp.concatenate([low[4:6], here, high[4:6]], axis=0)
        speed = jnp.concatenate([low[1:2], zonal_ref[l], high[0:2]], axis=0)
        mixing = jnp.concatenate([low[3:4], lateral_ref[l], high[2:4]], axis=0)
        opened = wets[:-1] * wets[1:]
        opened_all[0, l] = opened[1 : columns + 1]
        spread_rows(zonal_fields, (l,), opened, speed, mixing, columns + 3)
        return carry

    lax.fori_loop(0, levels, zonal_build, 0)

    def vert_build(row, carry):
        level = lev * levels + row - 1
        opened = wet(level - 1) * wet(level)
        spread_rows(
            vert_fields, (row,), opened, vert_ext[row + 1], vmix_ext[row + 1], columns
        )
        return carry

    lax.fori_loop(0, levels + 3, vert_build, 0)

    def vert_opened(l, carry):
        level = lev * levels + l
        opened_all[2, l] = wet(level - 1) * wet(level)
        return carry

    lax.fori_loop(0, levels, vert_opened, 0)

    def forward_zonal(g):
        def step(l, carry):
            def emit(x, value):
                middle[g, l + 2, x + 2] += value

            forward_line(
                columns,
                lambda x: first[g, l + 2, x + 2],
                lambda c: zonal_fields[0, l, c + 1],
                lambda c: zonal_fields[1, l, c + 1],
                lambda c: zonal_fields[2, l, c + 1],
                emit,
            )
            return carry

        lax.fori_loop(0, levels, step, 0)

    def forward_vert(g):
        def step(i, carry):
            def emit(x, value):
                middle[g, x + 2, i + 2] += value

            forward_line(
                levels,
                lambda x: first[g, x + 2, i + 2],
                lambda c: vert_fields[0, c + 1, i],
                lambda c: vert_fields[1, c + 1, i],
                lambda c: vert_fields[2, c + 1, i],
                emit,
            )
            return carry

        lax.fori_loop(0, columns, step, 0)

    def pull_merid(state, cot, store, g, fresh):
        def step(l, carry):
            for i in range(columns):
                own_cot = cot[g, l + 2, i + 2]
                pulled, share = backward_cell(
                    state[g, l + 2, i + 2],
                    own_cot,
                    merid_fields[0, l, i],
                    merid_fields[1, l, i],
                    merid_fields[2, l, i],
                    lane,
                    end,
                )
                store(g, l, i, own_cot + pulled, True)
                sums[1, l, i] = share if fresh else sums[1, l, i] + share
            return carry

        lax.fori_loop(0, levels, step, 0)

    def pull_zonal(state, cot, store, g, fresh):
        def step(l, carry):
            def speed(c, value):
                sums[0, l, c] = value if fresh else sums[0, l, c] + value

            backward_line(
                columns,
                lambda x: state[g, l + 2, x + 2],
                lambda x: cot[g, l + 2, x + 2],
                lambda c: zonal_fields[0, l, c + 1],
                lambda c: zonal_fields[1, l, c + 1],
                lambda c: zonal_fields[2, l, c + 1],
                lambda x, value: store(g, l, x, value, False),
                speed,
            )
            return carry

        lax.fori_loop(0, levels, step, 0)

    def pull_vert(state, cot, store, g, fresh):
        def step(i, carry):
            def speed(c, value):
                sums[2, c, i] = value if fresh else sums[2, c, i] + value

            backward_line(
                levels,
                lambda x: state[g, x + 2, i + 2],
                lambda x: cot[g, x + 2, i + 2],
                lambda c: vert_fields[0, c + 1, i],
                lambda c: vert_fields[1, c + 1, i],
                lambda c: vert_fields[2, c + 1, i],
                lambda x, value: store(g, x, i, value, False),
                speed,
            )
            return carry

        lax.fori_loop(0, columns, step, 0)

    def store_middle(g, l, i, value, fresh):
        if fresh:
            middle_cot[g, l + 2, i + 2] = value
        else:
            middle_cot[g, l + 2, i + 2] += value

    def store_start(g, l, i, value, fresh):
        rows = pl.ds(g * ROWS * cells + l * columns + i, ROWS, stride=cells)
        if fresh:
            start_ref[rows, :] = value
        else:
            start_ref[rows, :] = start_ref[rows, :] + value

    for g in range(groups):
        arrive(first_copies[g])
        forward_zonal(g)
        forward_vert(g)
        start(middle_copies[g])
    for g in range(groups):
        pull_merid(middle, last_cot, store_middle, g, g == 0)
    for g in range(groups):
        arrive(cot_copies[g])
        arrive(middle_copies[g])
        pull_zonal(middle, last_cot, store_middle, g, g == 0)
        pull_vert(middle, last_cot, store_middle, g, g == 0)
        start(back_copies[g])
    for g in range(groups):
        pull_merid(first, middle_cot, store_start, g, False)
    for g in range(groups):
        arrive(back_copies[g])
        pull_zonal(first, middle_cot, store_start, g, False)
        pull_vert(first, middle_cot, store_start, g, False)

    def reduce_level(l, carry):
        for row in range(3):
            reduced[row, l] = opened_all[row, l] * jnp.sum(sums[row, l], axis=1)
        return carry

    lax.fori_loop(0, levels, reduce_level, 0)
    share = levels // groups_trc
    sum_copies = []
    for step in range(1, groups_trc):
        target = lax.rem(trc + step, groups_trc)
        copy = pltpu.make_async_remote_copy(
            src_ref=reduced.at[:, pl.ds(target * share, share)],
            dst_ref=arrived.at[step - 1],
            send_sem=sum_send.at[step - 1],
            recv_sem=sum_recv.at[step - 1],
            device_id={"trc": target},
            device_id_type=MESH,
        )
        copy.start()
        sum_copies.append(copy)
    total = reduced[:, pl.ds(trc * share, share)]
    for step, copy in enumerate(sum_copies):
        copy.wait_recv()
        total = total + arrived[step]
    speed_ref[...] = total

    for copies in [field_copies] + first_copies + cot_copies + middle_copies + back_copies:
        finish(copies)
    for copy in sum_copies:
        copy.wait_send()


def body(sizes, tracers, cotangent, *fields):
    count, levels, columns, lanes = tracers.shape
    groups = count // ROWS
    share = levels // sizes[2]
    extended = pltpu.VMEM((groups, levels + 4, columns + 4, ROWS, lanes), jnp.float32)
    flat = (count * levels * columns, lanes)
    start_cot, speed_cot = pl.pallas_call(
        functools.partial(kernel, sizes, tracers.shape),
        out_shape=(
            jax.ShapeDtypeStruct(flat, jnp.float32),
            jax.ShapeDtypeStruct((3, share, columns, lanes), jnp.float32),
        ),
        in_specs=[pl.BlockSpec(memory_space=pltpu.VMEM)] * 8,
        out_specs=(pl.BlockSpec(memory_space=pltpu.VMEM),) * 2,
        scratch_shapes=[
            extended,
            extended,
            extended,
            extended,
            pltpu.VMEM((2, levels, 8, lanes), jnp.float32),
            pltpu.VMEM((2, levels, 8, lanes), jnp.float32),
            pltpu.VMEM((levels + 4, columns, lanes), jnp.float32),
            pltpu.VMEM((levels + 4, columns, lanes), jnp.float32),
            pltpu.VMEM((3, levels, columns + 3, ROWS, lanes), jnp.float32),
            pltpu.VMEM((3, levels + 3, columns, ROWS, lanes), jnp.float32),
            pltpu.VMEM((3, levels, columns, ROWS, lanes), jnp.float32),
            pltpu.VMEM((3, levels, columns, lanes), jnp.float32),
            pltpu.VMEM((3, levels, columns, ROWS, lanes), jnp.float32),
            pltpu.VMEM((3, levels, columns, lanes), jnp.float32),
            pltpu.VMEM((max(sizes[2] - 1, 1), 3, share, columns, lanes), jnp.float32),
            pltpu.SemaphoreType.DMA((4, groups, 4)),
            pltpu.SemaphoreType.DMA((4, groups, 4)),
            pltpu.SemaphoreType.DMA((2, 4)),
            pltpu.SemaphoreType.DMA((2, 4)),
            pltpu.SemaphoreType.DMA((max(sizes[2] - 1, 1),)),
            pltpu.SemaphoreType.DMA((max(sizes[2] - 1, 1),)),
        ],
        compiler_params=pltpu.CompilerParams(
            collective_id=0, has_side_effects=True, vmem_limit_bytes=48 * 1024 * 1024
        ),
    )(tracers.reshape(flat), cotangent.reshape(flat), *fields)
    return start_cot.reshape(tracers.shape), speed_cot


def solution(mesh):
    sizes = (mesh.shape["tile"], mesh.shape["lev"], mesh.shape["trc"])
    return jax.shard_map(
        functools.partial(body, sizes),
        mesh=mesh,
        in_specs=(
            P("trc", "lev", ("ens", "tile"), None),
            P("trc", "lev", ("ens", "tile"), None),
            P("lev", ("ens", "tile"), None),
            P("lev", ("ens", "tile"), None),
            P("lev", ("ens", "tile"), None),
            P("lev", ("ens", "tile"), None),
            P("lev", ("ens", "tile"), None),
            P(("ens", "tile"), None),
        ),
        out_specs=(
            P("trc", "lev", ("ens", "tile"), None),
            P(None, ("lev", "trc"), ("ens", "tile"), None),
        ),
        check_vma=False,
    )
```

```python
import functools

import jax
import jax.numpy as jnp
from jax import lax
from jax.experimental import pallas as pl
from jax.experimental.pallas import tpu as pltpu
from jax.sharding import PartitionSpec as P

ALBADA_FLOOR = 0.01
MESH = pl.DeviceIdType.MESH
ROWS = 8


def inverse(values):
    return pl.reciprocal(values, approx=True)


def limiter(lower, upper, lower_square, upper_square):
    half_inverse = inverse(lower_square + upper_square)
    product = lower * upper
    total = lower + upper
    return product * total * half_inverse, half_inverse, total


def doubled_square(step):
    return step * (step + step) + ALBADA_FLOOR


def forward_line(count, q, rise, fall, spread, emit):
    values = {x: q(x) for x in range(-2, count + 2)}
    steps = {c: values[c] - values[c - 1] for c in range(-1, count + 2)}
    squares = {c: doubled_square(steps[c]) for c in steps}
    through = {}
    above = None
    for x in range(-1, count + 1):
        slope, _, _ = limiter(steps[x], steps[x + 1], squares[x], squares[x + 1])
        if x >= 0:
            through[x] = (
                rise(x) * above + fall(x) * (values[x] - slope) - spread(x) * steps[x]
            )
        above = values[x] + slope
        if x >= 1:
            emit(x - 1, through[x - 1] - through[x])


def backward_line(count, q, g, rise, fall, spread, emit, speed):
    values = {x: q(x) for x in range(-2, count + 2)}
    steps = {c: values[c] - values[c - 1] for c in range(-1, count + 2)}
    squares = {c: doubled_square(steps[c]) for c in steps}
    cots = {x: g(x) for x in range(-2, count + 2)}
    up, down, jump, falls = {}, {}, {}, {}
    faces = {c: cots[c] - cots[c - 1] for c in range(-1, count + 2)}
    for c in range(0, count + 2):
        up[c] = faces[c] * rise(c)
    for c in range(-1, count + 1):
        falls[c] = fall(c)
        down[c] = faces[c] * falls[c]
    above, later = None, None
    for x in range(-1, count + 1):
        lower, upper = steps[x], steps[x + 1]
        slope, half_inverse, total = limiter(lower, upper, squares[x], squares[x + 1])
        weight = half_inverse * (up[x + 1] - down[x])
        fourfold = 4.0 * slope
        if x >= 0:
            first = (upper * (lower + total) - lower * fourfold) * weight
            jump[x] = first + later - spread(x) * faces[x]
        if x < count:
            later = (lower * (upper + total) - upper * fourfold) * weight
        if 0 <= x < count:
            carried = jnp.where(falls[x] < 0.0, values[x] - slope, above)
            speed(x, faces[x] * carried)
        above = values[x] + slope
        if x >= 1:
            emit(x - 1, (jump[x - 1] - jump[x]) + (up[x] + down[x - 1]))


def across(values, lane, last):
    before = jnp.where(lane == 0, 0.0, pltpu.roll(values, 1, 1))
    lower = values - before
    upper = jnp.where(lane == last, -values, pltpu.roll(lower, last, 1))
    return lower, upper


def forward_cell(values, rise, fall, spread, lane, last):
    lower, upper = across(values, lane, last)
    slope, _, _ = limiter(lower, upper, doubled_square(lower), doubled_square(upper))
    above = pltpu.roll(values + slope, 1, 1)
    through = rise * above + fall * (values - slope) - spread * lower
    return through - pltpu.roll(through, last, 1)


def backward_cell(values, cot, rise, fall, spread, lane, last):
    lower, upper = across(values, lane, last)
    slope, half_inverse, total = limiter(
        lower, upper, doubled_square(lower), doubled_square(upper)
    )
    face = cot - pltpu.roll(cot, 1, 1)
    up = pltpu.roll(face * rise, last, 1)
    down = face * fall
    weight = half_inverse * (up - down)
    fourfold = 4.0 * slope
    first = (upper * (lower + total) - lower * fourfold) * weight
    later = (lower * (upper + total) - upper * fourfold) * weight
    near = first - spread * face
    result = (
        near
        - later
        + up
        + down
        + jnp.where(lane == 0, 0.0, pltpu.roll(later, 1, 1))
        - jnp.where(lane == last, 0.0, pltpu.roll(near, last, 1))
    )
    carried = jnp.where(fall < 0.0, values - slope, pltpu.roll(values + slope, 1, 1))
    return result, face * carried


def kernel(
    sizes,
    dims,
    tracer_hbm,
    cot_hbm,
    zonal_hbm,
    merid_hbm,
    vert_hbm,
    lateral_hbm,
    vmix_hbm,
    depth_hbm,
    start_ref,
    speed_ref,
    first,
    last_cot,
    middle,
    middle_cot,
    pack,
    packed,
    vert_ext,
    vmix_ext,
    zonal_fields,
    vert_fields,
    merid_fields,
    opened_all,
    sums,
    reduced,
    arrived,
    halo_send,
    halo_recv,
    field_send,
    field_recv,
    sum_send,
    sum_recv,
    start_sum,
    load_sem,
    *loaded,
):
    outside = (
        tracer_hbm,
        cot_hbm,
        zonal_hbm,
        merid_hbm,
        vert_hbm,
        lateral_hbm,
        vmix_hbm,
        depth_hbm,
    )
    loads = [
        pltpu.make_async_copy(source, target, load_sem.at[row])
        for row, (source, target) in enumerate(zip(outside, loaded))
    ]
    for load in loads:
        load.start()
    (
        tracer_ref,
        cot_ref,
        zonal_ref,
        merid_ref,
        vert_ref,
        lateral_ref,
        vmix_ref,
        depth_ref,
    ) = loaded
    tiles, levs, groups_trc = sizes
    tracers, levels, columns, lanes = dims
    groups = tracers // ROWS
    end = lanes - 1
    cells = levels * columns
    tile, lev, trc = lax.axis_index("tile"), lax.axis_index("lev"), lax.axis_index("trc")
    lane = lax.broadcasted_iota(jnp.int32, (ROWS, lanes), 1)

    below = {"tile": tile > 0, "lev": lev > 0}
    beyond = {"tile": tile < tiles - 1, "lev": lev < levs - 1}
    place = {"tile": tile, "lev": lev}
    size = {"tile": tiles, "lev": levs}
    axes = [axis for axis in ("tile", "lev") if size[axis] > 1]

    barrier = pltpu.get_barrier_semaphore()
    expected = groups_trc - 1
    for axis in axes:
        for there, offset in ((below[axis], -1), (beyond[axis], 1)):

            @pl.when(there)
            def _(axis=axis, offset=offset):
                pl.semaphore_signal(
                    barrier,
                    inc=1,
                    device_id={axis: place[axis] + offset},
                    device_id_type=MESH,
                )

            expected = expected + there.astype(jnp.int32)
    for step in range(1, groups_trc):
        pl.semaphore_signal(
            barrier,
            inc=1,
            device_id={"trc": lax.rem(trc + step, groups_trc)},
            device_id_type=MESH,
        )

    def wet(level):
        known = jnp.logical_and(level < depth_ref[...], level >= 0)
        return jnp.where(known, 1.0, 0.0)

    def load_own(l, carry):
        for g in range(groups):
            for i in range(columns):
                rows = pl.ds(g * ROWS * cells + l * columns + i, ROWS, stride=cells)
                first[g, l + 2, i + 2] = tracer_ref[rows, :]
                last_cot[g, l + 2, i + 2] = cot_ref[rows, :]
        here = wet(lev * levels + l)
        zonal, lateral = zonal_ref[l], lateral_ref[l]
        for side, rows in ((0, slice(0, 2)), (1, slice(columns - 2, columns))):
            pack[side, l] = jnp.concatenate(
                [zonal[rows], lateral[rows], here[rows], here[rows]], axis=0
            )
        vert_ext[l + 2] = vert_ref[l]
        vmix_ext[l + 2] = vmix_ref[l]
        return carry

    zero_tile = jnp.zeros((ROWS, lanes), jnp.float32)

    def clear(side):
        for buffer in (first, last_cot, middle, middle_cot):
            for g in range(groups):
                if side < 2:
                    place_at = columns + 2 if side == 0 else 0

                    def clear_row(l, carry):
                        buffer[g, l + 2, place_at] = zero_tile
                        buffer[g, l + 2, place_at + 1] = zero_tile
                        return carry

                    lax.fori_loop(0, levels, clear_row, 0)
                else:
                    place_at = levels + 2 if side == 2 else 0

                    def clear_column(i, carry):
                        buffer[g, place_at, i + 2] = zero_tile
                        buffer[g, place_at + 1, i + 2] = zero_tile
                        return carry

                    lax.fori_loop(0, columns, clear_column, 0)
        if side < 2:
            packed[side] = jnp.zeros_like(packed[side])
        else:
            place_at = levels + 2 if side == 2 else 0
            for buffer in (vert_ext, vmix_ext):
                buffer[place_at] = zero_tile_rows
                buffer[place_at + 1] = zero_tile_rows

    zero_tile_rows = jnp.zeros((columns, lanes), jnp.float32)
    for side, axis, there in (
        (0, "tile", beyond["tile"]),
        (1, "tile", below["tile"]),
        (2, "lev", beyond["lev"]),
        (3, "lev", below["lev"]),
    ):
        if size[axis] > 1:

            @pl.when(jnp.logical_not(there))
            def _(side=side):
                clear(side)

        else:
            clear(side)

    for load in loads:
        load.wait()
    lax.fori_loop(0, levels, load_own, 0)

    pl.semaphore_wait(barrier, expected)

    def exchange(pairs, send_sem, recv_sem):
        copies = []
        for side, source, destination in pairs:
            axis = "tile" if side in (0, 1) else "lev"
            if size[axis] == 1:
                continue
            goes_down = side in (0, 2)
            copy = pltpu.make_async_remote_copy(
                src_ref=source,
                dst_ref=destination,
                send_sem=send_sem(side),
                recv_sem=recv_sem(side),
                device_id={axis: place[axis] + (-1 if goes_down else 1)},
                device_id_type=MESH,
            )
            sends = below[axis] if goes_down else beyond[axis]
            receives = beyond[axis] if goes_down else below[axis]
            copies.append((copy, sends, receives, axis))
        return copies

    def start(copies):
        for copy, sends, _, _ in copies:
            pl.when(sends)(copy.start)

    def arrive(copies, along=("tile", "lev")):
        for copy, _, receives, axis in copies:
            if axis in along:
                pl.when(receives)(copy.wait_recv)

    def finish(copies):
        for copy, sends, _, _ in copies:
            pl.when(sends)(copy.wait_send)

    own_l, own_i = pl.ds(2, levels), pl.ds(2, columns)

    def halo(buffer, stage, g):
        pairs = [
            (0, buffer.at[g, own_l, pl.ds(2, 2)], buffer.at[g, own_l, pl.ds(columns + 2, 2)]),
            (1, buffer.at[g, own_l, pl.ds(columns, 2)], buffer.at[g, own_l, pl.ds(0, 2)]),
            (2, buffer.at[g, pl.ds(2, 2), own_i], buffer.at[g, pl.ds(levels + 2, 2), own_i]),
            (3, buffer.at[g, pl.ds(levels, 2), own_i], buffer.at[g, pl.ds(0, 2), own_i]),
        ]
        return exchange(
            pairs,
            lambda side: halo_send.at[stage, g, side],
            lambda side: halo_recv.at[stage, g, side],
        )

    field_copies = exchange(
        [(0, pack.at[0], packed.at[0]), (1, pack.at[1], packed.at[1])],
        lambda side: field_send.at[0, side],
        lambda side: field_recv.at[0, side],
    )
    for row, buffer in enumerate((vert_ext, vmix_ext)):
        field_copies += exchange(
            [
                (2, buffer.at[pl.ds(2, 2)], buffer.at[pl.ds(levels + 2, 2)]),
                (3, buffer.at[pl.ds(levels, 2)], buffer.at[pl.ds(0, 2)]),
            ],
            lambda side, row=row: field_send.at[row, side],
            lambda side, row=row: field_recv.at[row, side],
        )
    first_copies = [halo(first, 0, g) for g in range(groups)]
    cot_copies = [halo(last_cot, 1, g) for g in range(groups)]
    middle_copies = [halo(middle, 2, g) for g in range(groups)]
    back_copies = [halo(middle_cot, 3, g) for g in range(groups)]

    start(first_copies[0])
    start(field_copies)
    for copies in first_copies[1:] + cot_copies:
        start(copies)

    def spread_rows(target, head, opened, speed, mixing, count):
        kinds = (
            opened * jnp.maximum(speed, 0.0),
            opened * jnp.minimum(speed, 0.0),
            opened * mixing,
        )
        for kind, values in enumerate(kinds):
            for i in range(count):
                target[(kind,) + head + (i,)] = jnp.broadcast_to(
                    values[i : i + 1], (ROWS, lanes)
                )

    def merid_build(l, carry):
        here = wet(lev * levels + l)
        south = jnp.where(lane[:columns] == 0, 0.0, pltpu.roll(here, 1, 1))
        opened = here * south
        opened_all[1, l] = opened
        spread_rows(merid_fields, (l,), opened, merid_ref[l], lateral_ref[l], columns)
        return carry

    lax.fori_loop(0, levels, merid_build, 0)

    def forward_merid(g):
        def step(l, carry):
            for i in range(columns):
                values = first[g, l + 2, i + 2]
                middle[g, l + 2, i + 2] = values + forward_cell(
                    values,
                    merid_fields[0, l, i],
                    merid_fields[1, l, i],
                    merid_fields[2, l, i],
                    lane,
                    end,
                )
            return carry

        lax.fori_loop(0, levels, step, 0)

    for g in range(groups):
        forward_merid(g)

    def zonal_build(l, carry):
        low, high = packed[1, l], packed[0, l]
        here = wet(lev * levels + l)
        wets = jnp.concatenate([low[4:6], here, high[4:6]], axis=0)
        speed = jnp.concatenate([low[1:2], zonal_ref[l], high[0:2]], axis=0)
        mixing = jnp.concatenate([low[3:4], lateral_ref[l], high[2:4]], axis=0)
        opened = wets[:-1] * wets[1:]
        opened_all[0, l] = opened[1 : columns + 1]
        spread_rows(zonal_fields, (l,), opened, speed, mixing, columns + 3)
        return carry

    def vert_build(row, carry):
        level = lev * levels + row - 1
        opened = wet(level - 1) * wet(level)
        spread_rows(
            vert_fields, (row,), opened, vert_ext[row + 1], vmix_ext[row + 1], columns
        )
        return carry

    def vert_opened(l, carry):
        level = lev * levels + l
        opened_all[2, l] = wet(level - 1) * wet(level)
        return carry

    def forward_zonal(g):
        def step(l, carry):
            def emit(x, value):
                middle[g, l + 2, x + 2] += value

            forward_line(
                columns,
                lambda x: first[g, l + 2, x + 2],
                lambda c: zonal_fields[0, l, c + 1],
                lambda c: zonal_fields[1, l, c + 1],
                lambda c: zonal_fields[2, l, c + 1],
                emit,
            )
            return carry

        lax.fori_loop(0, levels, step, 0)

    def forward_vert(g):
        def step(i, carry):
            def emit(x, value):
                middle[g, x + 2, i + 2] += value

            forward_line(
                levels,
                lambda x: first[g, x + 2, i + 2],
                lambda c: vert_fields[0, c + 1, i],
                lambda c: vert_fields[1, c + 1, i],
                lambda c: vert_fields[2, c + 1, i],
                emit,
            )
            return carry

        lax.fori_loop(0, columns, step, 0)

    def pull_merid(state, cot, store, g, fresh):
        def step(l, carry):
            for i in range(columns):
                own_cot = cot[g, l + 2, i + 2]
                pulled, share = backward_cell(
                    state[g, l + 2, i + 2],
                    own_cot,
                    merid_fields[0, l, i],
                    merid_fields[1, l, i],
                    merid_fields[2, l, i],
                    lane,
                    end,
                )
                store(g, l, i, own_cot + pulled, True)
                sums[1, l, i] = share if fresh else sums[1, l, i] + share
            return carry

        lax.fori_loop(0, levels, step, 0)

    def pull_zonal(state, cot, store, g, fresh, begin=0, count=levels):
        def step(index, carry):
            l = lax.rem(begin + index, levels)

            def speed(c, value):
                sums[0, l, c] = value if fresh else sums[0, l, c] + value

            backward_line(
                columns,
                lambda x: state[g, l + 2, x + 2],
                lambda x: cot[g, l + 2, x + 2],
                lambda c: zonal_fields[0, l, c + 1],
                lambda c: zonal_fields[1, l, c + 1],
                lambda c: zonal_fields[2, l, c + 1],
                lambda x, value: store(g, l, x, value, False),
                speed,
            )
            return carry

        lax.fori_loop(0, count, step, 0)

    def pull_vert(state, cot, store, g, fresh):
        def step(i, carry):
            def speed(c, value):
                sums[2, c, i] = value if fresh else sums[2, c, i] + value

            backward_line(
                levels,
                lambda x: state[g, x + 2, i + 2],
                lambda x: cot[g, x + 2, i + 2],
                lambda c: vert_fields[0, c + 1, i],
                lambda c: vert_fields[1, c + 1, i],
                lambda c: vert_fields[2, c + 1, i],
                lambda x, value: store(g, x, i, value, False),
                speed,
            )
            return carry

        lax.fori_loop(0, columns, step, 0)

    def store_middle(g, l, i, value, fresh):
        if fresh:
            middle_cot[g, l + 2, i + 2] = value
        else:
            middle_cot[g, l + 2, i + 2] += value

    def store_start(g, l, i, value, fresh):
        if fresh:
            start_sum[g, l, i] = value
        else:
            start_sum[g, l, i] += value

    def store_last(g, l, i, value, fresh):
        rows = pl.ds(g * ROWS * cells + l * columns + i, ROWS, stride=cells)
        start_ref[rows, :] = start_sum[g, l, i] + value

    for g in range(groups):
        arrive(first_copies[g], ("lev",))
        if g == 0:
            arrive(field_copies)
            lax.fori_loop(0, levels, zonal_build, 0)
            lax.fori_loop(0, levels + 3, vert_build, 0)
            lax.fori_loop(0, levels, vert_opened, 0)
        forward_vert(g)
        arrive(first_copies[g], ("tile",))
        forward_zonal(g)
        start(middle_copies[g])
    for g in range(groups):
        pull_merid(middle, last_cot, store_middle, g, g == 0)
    for g in range(groups):
        arrive(cot_copies[g])
        arrive(middle_copies[g], ("lev",))
        pull_vert(middle, last_cot, store_middle, g, g == 0)
        arrive(middle_copies[g], ("tile",))
        pull_zonal(middle, last_cot, store_middle, g, g == 0)
        start(back_copies[g])
    for g in range(groups):
        pull_merid(first, middle_cot, store_start, g, False)
    for g in range(groups):
        arrive(back_copies[g], ("lev",))
        pull_vert(first, middle_cot, store_start, g, False)

    share = levels // groups_trc
    sum_copies = []

    def reduce_rows(rows, begin, count):
        def step(index, carry):
            l = lax.rem(begin + index, levels)
            for row in rows:
                reduced[row, l] = opened_all[row, l] * jnp.sum(sums[row, l], axis=1)
            return carry

        lax.fori_loop(0, count, step, 0)

    def send_rows(part, rows):
        for step in range(1, groups_trc):
            target = lax.rem(trc + step, groups_trc)
            copy = pltpu.make_async_remote_copy(
                src_ref=reduced.at[rows, pl.ds(target * share, share)],
                dst_ref=arrived.at[step - 1, rows],
                send_sem=sum_send.at[part, step - 1],
                recv_sem=sum_recv.at[part, step - 1],
                device_id={"trc": target},
                device_id_type=MESH,
            )
            copy.start()
            sum_copies.append(copy)

    reduce_rows((1, 2), 0, levels)
    send_rows(0, pl.ds(1, 2))
    for g in range(groups):
        arrive(back_copies[g], ("tile",))
    after = (trc + 1) * share
    if groups_trc > 1:
        for g in range(groups):
            pull_zonal(first, middle_cot, store_last, g, False, after, levels - share)
        reduce_rows((0,), after, levels - share)
        send_rows(1, pl.ds(0, 1))
    for g in range(groups):
        pull_zonal(first, middle_cot, store_last, g, False, trc * share, share)
    reduce_rows((0,), trc * share, share)
    total = reduced[:, pl.ds(trc * share, share)]
    for copy in sum_copies:
        copy.wait_recv()
    for step in range(1, groups_trc):
        total = total + arrived[step - 1]
    speed_ref[...] = total

    for copies in [field_copies] + first_copies + cot_copies + middle_copies + back_copies:
        finish(copies)
    for copy in sum_copies:
        copy.wait_send()


def body(sizes, tracers, cotangent, *fields):
    count, levels, columns, lanes = tracers.shape
    groups = count // ROWS
    share = levels // sizes[2]
    extended = pltpu.VMEM((groups, levels + 4, columns + 4, ROWS, lanes), jnp.float32)
    flat = (count * levels * columns, lanes)
    start_cot, speed_cot = pl.pallas_call(
        functools.partial(kernel, sizes, tracers.shape),
        out_shape=(
            jax.ShapeDtypeStruct(flat, jnp.float32),
            jax.ShapeDtypeStruct((3, share, columns, lanes), jnp.float32),
        ),
        in_specs=[pl.BlockSpec(memory_space=pltpu.HBM)] * 8,
        out_specs=(pl.BlockSpec(memory_space=pltpu.VMEM),) * 2,
        scratch_shapes=[
            extended,
            extended,
            extended,
            extended,
            pltpu.VMEM((2, levels, 8, lanes), jnp.float32),
            pltpu.VMEM((2, levels, 8, lanes), jnp.float32),
            pltpu.VMEM((levels + 4, columns, lanes), jnp.float32),
            pltpu.VMEM((levels + 4, columns, lanes), jnp.float32),
            pltpu.VMEM((3, levels, columns + 3, ROWS, lanes), jnp.float32),
            pltpu.VMEM((3, levels + 3, columns, ROWS, lanes), jnp.float32),
            pltpu.VMEM((3, levels, columns, ROWS, lanes), jnp.float32),
            pltpu.VMEM((3, levels, columns, lanes), jnp.float32),
            pltpu.VMEM((3, levels, columns, ROWS, lanes), jnp.float32),
            pltpu.VMEM((3, levels, columns, lanes), jnp.float32),
            pltpu.VMEM((max(sizes[2] - 1, 1), 3, share, columns, lanes), jnp.float32),
            pltpu.SemaphoreType.DMA((4, groups, 4)),
            pltpu.SemaphoreType.DMA((4, groups, 4)),
            pltpu.SemaphoreType.DMA((2, 4)),
            pltpu.SemaphoreType.DMA((2, 4)),
            pltpu.SemaphoreType.DMA((2, max(sizes[2] - 1, 1))),
            pltpu.SemaphoreType.DMA((2, max(sizes[2] - 1, 1))),
            pltpu.VMEM((groups, levels, columns, ROWS, lanes), jnp.float32),
            pltpu.SemaphoreType.DMA((8,)),
            pltpu.VMEM(flat, jnp.float32),
            pltpu.VMEM(flat, jnp.float32),
            *[pltpu.VMEM(values.shape, values.dtype) for values in fields],
        ],
        compiler_params=pltpu.CompilerParams(
            collective_id=0, has_side_effects=True, vmem_limit_bytes=48 * 1024 * 1024
        ),
    )(tracers.reshape(flat), cotangent.reshape(flat), *fields)
    return start_cot.reshape(tracers.shape), speed_cot


def solution(mesh):
    sizes = (mesh.shape["tile"], mesh.shape["lev"], mesh.shape["trc"])
    return jax.shard_map(
        functools.partial(body, sizes),
        mesh=mesh,
        in_specs=(
            P("trc", "lev", ("ens", "tile"), None),
            P("trc", "lev", ("ens", "tile"), None),
            P("lev", ("ens", "tile"), None),
            P("lev", ("ens", "tile"), None),
            P("lev", ("ens", "tile"), None),
            P("lev", ("ens", "tile"), None),
            P("lev", ("ens", "tile"), None),
            P(("ens", "tile"), None),
        ),
        out_specs=(
            P("trc", "lev", ("ens", "tile"), None),
            P(None, ("lev", "trc"), ("ens", "tile"), None),
        ),
        check_vma=False,
    )
```

```python
import functools

import jax
import jax.numpy as jnp
from jax import lax
from jax.experimental import pallas as pl
from jax.experimental.pallas import tpu as pltpu
from jax.sharding import PartitionSpec as P

ALBADA_FLOOR = 0.01
MESH = pl.DeviceIdType.MESH
ROWS = 8


def inverse(values):
    return pl.reciprocal(values, approx=True)


def limiter(lower, upper, lower_square, upper_square):
    half_inverse = inverse(lower_square + upper_square)
    product = lower * upper
    total = lower + upper
    return product * total * half_inverse, half_inverse, total


def doubled_square(step):
    return step * (step + step) + ALBADA_FLOOR


def slopes(lower, upper, slope, half_inverse, total):
    fourfold = 4.0 * slope
    by_lower = (upper * (lower + total) - lower * fourfold) * half_inverse
    by_upper = (lower * (upper + total) - upper * fourfold) * half_inverse
    return by_lower, by_upper


def forward_line(count, q, rise, fall, spread, emit, keep, keep_face):
    values = {x: q(x) for x in range(-2, count + 2)}
    steps = {c: values[c] - values[c - 1] for c in range(-1, count + 2)}
    squares = {c: doubled_square(steps[c]) for c in steps}
    through = {}
    above = None
    for x in range(-1, count + 1):
        parts = limiter(steps[x], steps[x + 1], squares[x], squares[x + 1])
        slope = parts[0]
        keep(x, *slopes(steps[x], steps[x + 1], *parts))
        if x >= 0:
            falls = fall(x)
            carried = jnp.where(falls < 0.0, values[x] - slope, above)
            through[x] = (rise(x) + falls) * carried - spread(x) * steps[x]
            if x < count:
                keep_face(x, carried)
        above = values[x] + slope
        if x >= 1:
            emit(x - 1, through[x - 1] - through[x])


def backward_line(count, q, g, rise, fall, spread, emit, speed):
    values = {x: q(x) for x in range(-2, count + 2)}
    steps = {c: values[c] - values[c - 1] for c in range(-1, count + 2)}
    squares = {c: doubled_square(steps[c]) for c in steps}
    cots = {x: g(x) for x in range(-2, count + 2)}
    up, down, jump, falls = {}, {}, {}, {}
    faces = {c: cots[c] - cots[c - 1] for c in range(-1, count + 2)}
    for c in range(0, count + 2):
        up[c] = faces[c] * rise(c)
    for c in range(-1, count + 1):
        falls[c] = fall(c)
        down[c] = faces[c] * falls[c]
    above, later = None, None
    for x in range(-1, count + 1):
        lower, upper = steps[x], steps[x + 1]
        slope, half_inverse, total = limiter(lower, upper, squares[x], squares[x + 1])
        weight = half_inverse * (up[x + 1] - down[x])
        fourfold = 4.0 * slope
        if x >= 0:
            first = (upper * (lower + total) - lower * fourfold) * weight
            jump[x] = first + later - spread(x) * faces[x]
        if x < count:
            later = (lower * (upper + total) - upper * fourfold) * weight
        if 0 <= x < count:
            carried = jnp.where(falls[x] < 0.0, values[x] - slope, above)
            speed(x, faces[x] * carried)
        above = values[x] + slope
        if x >= 1:
            emit(x - 1, (jump[x - 1] - jump[x]) + (up[x] + down[x - 1]))


def early_line(count, g, kept, carried, rise, fall, spread, emit, speed):
    cots = {x: g(x) for x in range(-2, count + 2)}
    faces = {c: cots[c] - cots[c - 1] for c in range(-1, count + 2)}
    up = {c: faces[c] * rise(c) for c in range(0, count + 2)}
    down = {c: faces[c] * fall(c) for c in range(-1, count + 1)}
    jump, later = {}, None
    for x in range(-1, count + 1):
        weight = up[x + 1] - down[x]
        if x >= 0:
            jump[x] = kept(0, x) * weight + later - spread(x) * faces[x]
        if x < count:
            later = kept(1, x) * weight
        if 0 <= x < count:
            speed(x, faces[x] * carried(x))
        if x >= 1:
            emit(x - 1, (jump[x - 1] - jump[x]) + (up[x] + down[x - 1]))


def across(values, lane, last):
    before = jnp.where(lane == 0, 0.0, pltpu.roll(values, 1, 1))
    lower = values - before
    upper = jnp.where(lane == last, -values, pltpu.roll(lower, last, 1))
    return lower, upper


def forward_cell(values, rise, fall, spread, lane, last):
    lower, upper = across(values, lane, last)
    parts = limiter(lower, upper, doubled_square(lower), doubled_square(upper))
    slope = parts[0]
    above = pltpu.roll(values + slope, 1, 1)
    carried = jnp.where(fall < 0.0, values - slope, above)
    through = (rise + fall) * carried - spread * lower
    kept = slopes(lower, upper, *parts)
    return through - pltpu.roll(through, last, 1), kept, carried


def backward_cell(values, cot, rise, fall, spread, lane, last):
    lower, upper = across(values, lane, last)
    slope, half_inverse, total = limiter(
        lower, upper, doubled_square(lower), doubled_square(upper)
    )
    face = cot - pltpu.roll(cot, 1, 1)
    up = pltpu.roll(face * rise, last, 1)
    down = face * fall
    weight = half_inverse * (up - down)
    fourfold = 4.0 * slope
    first = (upper * (lower + total) - lower * fourfold) * weight
    later = (lower * (upper + total) - upper * fourfold) * weight
    near = first - spread * face
    result = (
        near
        - later
        + up
        + down
        + jnp.where(lane == 0, 0.0, pltpu.roll(later, 1, 1))
        - jnp.where(lane == last, 0.0, pltpu.roll(near, last, 1))
    )
    carried = jnp.where(fall < 0.0, values - slope, pltpu.roll(values + slope, 1, 1))
    return result, face * carried


def early_cell(cot, by_lower, by_upper, carried, rise, fall, spread, lane, last):
    face = cot - pltpu.roll(cot, 1, 1)
    up = pltpu.roll(face * rise, last, 1)
    down = face * fall
    weight = up - down
    later = by_upper * weight
    near = by_lower * weight - spread * face
    result = (
        near
        - later
        + up
        + down
        + jnp.where(lane == 0, 0.0, pltpu.roll(later, 1, 1))
        - jnp.where(lane == last, 0.0, pltpu.roll(near, last, 1))
    )
    return result, face * carried


def kernel(
    sizes,
    dims,
    tracer_hbm,
    cot_hbm,
    zonal_hbm,
    merid_hbm,
    vert_hbm,
    lateral_hbm,
    vmix_hbm,
    depth_hbm,
    start_ref,
    speed_ref,
    first,
    last_cot,
    middle,
    middle_cot,
    pack,
    packed,
    vert_ext,
    vmix_ext,
    zonal_fields,
    vert_fields,
    merid_fields,
    opened_all,
    sums,
    reduced,
    arrived,
    halo_send,
    halo_recv,
    field_send,
    field_recv,
    sum_send,
    sum_recv,
    start_sum,
    kept_zonal,
    kept_vert,
    kept_merid,
    carried_all,
    load_sem,
    *loaded,
):
    outside = (
        tracer_hbm,
        cot_hbm,
        zonal_hbm,
        merid_hbm,
        vert_hbm,
        lateral_hbm,
        vmix_hbm,
        depth_hbm,
    )
    loads = [
        pltpu.make_async_copy(source, target, load_sem.at[row])
        for row, (source, target) in enumerate(zip(outside, loaded))
    ]
    for load in loads:
        load.start()
    (
        tracer_ref,
        cot_ref,
        zonal_ref,
        merid_ref,
        vert_ref,
        lateral_ref,
        vmix_ref,
        depth_ref,
    ) = loaded
    tiles, levs, groups_trc = sizes
    tracers, levels, columns, lanes = dims
    groups = tracers // ROWS
    end = lanes - 1
    cells = levels * columns
    tile, lev, trc = lax.axis_index("tile"), lax.axis_index("lev"), lax.axis_index("trc")
    lane = lax.broadcasted_iota(jnp.int32, (ROWS, lanes), 1)

    below = {"tile": tile > 0, "lev": lev > 0}
    beyond = {"tile": tile < tiles - 1, "lev": lev < levs - 1}
    place = {"tile": tile, "lev": lev}
    size = {"tile": tiles, "lev": levs}
    axes = [axis for axis in ("tile", "lev") if size[axis] > 1]

    barrier = pltpu.get_barrier_semaphore()
    expected = groups_trc - 1
    for axis in axes:
        for there, offset in ((below[axis], -1), (beyond[axis], 1)):

            @pl.when(there)
            def _(axis=axis, offset=offset):
                pl.semaphore_signal(
                    barrier,
                    inc=1,
                    device_id={axis: place[axis] + offset},
                    device_id_type=MESH,
                )

            expected = expected + there.astype(jnp.int32)
    for step in range(1, groups_trc):
        pl.semaphore_signal(
            barrier,
            inc=1,
            device_id={"trc": lax.rem(trc + step, groups_trc)},
            device_id_type=MESH,
        )

    def wet(level):
        known = jnp.logical_and(level < depth_ref[...], level >= 0)
        return jnp.where(known, 1.0, 0.0)

    def load_own(l, carry):
        for g in range(groups):
            for i in range(columns):
                rows = pl.ds(g * ROWS * cells + l * columns + i, ROWS, stride=cells)
                first[g, l + 2, i + 2] = tracer_ref[rows, :]
                last_cot[g, l + 2, i + 2] = cot_ref[rows, :]
        here = wet(lev * levels + l)
        zonal, lateral = zonal_ref[l], lateral_ref[l]
        for side, rows in ((0, slice(0, 2)), (1, slice(columns - 2, columns))):
            pack[side, l] = jnp.concatenate(
                [zonal[rows], lateral[rows], here[rows], here[rows]], axis=0
            )
        vert_ext[l + 2] = vert_ref[l]
        vmix_ext[l + 2] = vmix_ref[l]
        return carry

    zero_tile = jnp.zeros((ROWS, lanes), jnp.float32)

    def clear(side):
        for buffer in (first, last_cot, middle, middle_cot):
            for g in range(groups):
                if side < 2:
                    place_at = columns + 2 if side == 0 else 0

                    def clear_row(l, carry):
                        buffer[g, l + 2, place_at] = zero_tile
                        buffer[g, l + 2, place_at + 1] = zero_tile
                        return carry

                    lax.fori_loop(0, levels, clear_row, 0)
                else:
                    place_at = levels + 2 if side == 2 else 0

                    def clear_column(i, carry):
                        buffer[g, place_at, i + 2] = zero_tile
                        buffer[g, place_at + 1, i + 2] = zero_tile
                        return carry

                    lax.fori_loop(0, columns, clear_column, 0)
        if side < 2:
            packed[side] = jnp.zeros_like(packed[side])
        else:
            place_at = levels + 2 if side == 2 else 0
            for buffer in (vert_ext, vmix_ext):
                buffer[place_at] = zero_tile_rows
                buffer[place_at + 1] = zero_tile_rows

    zero_tile_rows = jnp.zeros((columns, lanes), jnp.float32)
    for side, axis, there in (
        (0, "tile", beyond["tile"]),
        (1, "tile", below["tile"]),
        (2, "lev", beyond["lev"]),
        (3, "lev", below["lev"]),
    ):
        if size[axis] > 1:

            @pl.when(jnp.logical_not(there))
            def _(side=side):
                clear(side)

        else:
            clear(side)

    for load in loads:
        load.wait()
    lax.fori_loop(0, levels, load_own, 0)

    pl.semaphore_wait(barrier, expected)

    def exchange(pairs, send_sem, recv_sem):
        copies = []
        for side, source, destination in pairs:
            axis = "tile" if side in (0, 1) else "lev"
            if size[axis] == 1:
                continue
            goes_down = side in (0, 2)
            copy = pltpu.make_async_remote_copy(
                src_ref=source,
                dst_ref=destination,
                send_sem=send_sem(side),
                recv_sem=recv_sem(side),
                device_id={axis: place[axis] + (-1 if goes_down else 1)},
                device_id_type=MESH,
            )
            sends = below[axis] if goes_down else beyond[axis]
            receives = beyond[axis] if goes_down else below[axis]
            copies.append((copy, sends, receives, axis))
        return copies

    def start(copies):
        for copy, sends, _, _ in copies:
            pl.when(sends)(copy.start)

    def arrive(copies, along=("tile", "lev")):
        for copy, _, receives, axis in copies:
            if axis in along:
                pl.when(receives)(copy.wait_recv)

    def finish(copies):
        for copy, sends, _, _ in copies:
            pl.when(sends)(copy.wait_send)

    own_l, own_i = pl.ds(2, levels), pl.ds(2, columns)

    def halo(buffer, stage, g):
        pairs = [
            (0, buffer.at[g, own_l, pl.ds(2, 2)], buffer.at[g, own_l, pl.ds(columns + 2, 2)]),
            (1, buffer.at[g, own_l, pl.ds(columns, 2)], buffer.at[g, own_l, pl.ds(0, 2)]),
            (2, buffer.at[g, pl.ds(2, 2), own_i], buffer.at[g, pl.ds(levels + 2, 2), own_i]),
            (3, buffer.at[g, pl.ds(levels, 2), own_i], buffer.at[g, pl.ds(0, 2), own_i]),
        ]
        return exchange(
            pairs,
            lambda side: halo_send.at[stage, g, side],
            lambda side: halo_recv.at[stage, g, side],
        )

    field_copies = exchange(
        [(0, pack.at[0], packed.at[0]), (1, pack.at[1], packed.at[1])],
        lambda side: field_send.at[0, side],
        lambda side: field_recv.at[0, side],
    )
    for row, buffer in enumerate((vert_ext, vmix_ext)):
        field_copies += exchange(
            [
                (2, buffer.at[pl.ds(2, 2)], buffer.at[pl.ds(levels + 2, 2)]),
                (3, buffer.at[pl.ds(levels, 2)], buffer.at[pl.ds(0, 2)]),
            ],
            lambda side, row=row: field_send.at[row, side],
            lambda side, row=row: field_recv.at[row, side],
        )
    first_copies = [halo(first, 0, g) for g in range(groups)]
    cot_copies = [halo(last_cot, 1, g) for g in range(groups)]
    middle_copies = [halo(middle, 2, g) for g in range(groups)]
    back_copies = [halo(middle_cot, 3, g) for g in range(groups)]

    start(first_copies[0])
    start(field_copies)
    for copies in first_copies[1:] + cot_copies:
        start(copies)

    def spread_rows(target, head, opened, speed, mixing, count):
        kinds = (
            opened * jnp.maximum(speed, 0.0),
            opened * jnp.minimum(speed, 0.0),
            opened * mixing,
        )
        for kind, values in enumerate(kinds):
            for i in range(count):
                target[(kind,) + head + (i,)] = jnp.broadcast_to(
                    values[i : i + 1], (ROWS, lanes)
                )

    def merid_build(l, carry):
        here = wet(lev * levels + l)
        south = jnp.where(lane[:columns] == 0, 0.0, pltpu.roll(here, 1, 1))
        opened = here * south
        opened_all[1, l] = opened
        spread_rows(merid_fields, (l,), opened, merid_ref[l], lateral_ref[l], columns)
        return carry

    lax.fori_loop(0, levels, merid_build, 0)

    def forward_merid(g):
        def step(l, carry):
            for i in range(columns):
                values = first[g, l + 2, i + 2]
                gain, kept, carried = forward_cell(
                    values,
                    merid_fields[0, l, i],
                    merid_fields[1, l, i],
                    merid_fields[2, l, i],
                    lane,
                    end,
                )
                middle[g, l + 2, i + 2] = values + gain
                kept_merid[0, g, l, i] = kept[0]
                kept_merid[1, g, l, i] = kept[1]
                carried_all[1, g, l, i] = carried
            return carry

        lax.fori_loop(0, levels, step, 0)

    for g in range(groups):
        forward_merid(g)

    def zonal_build(l, carry):
        low, high = packed[1, l], packed[0, l]
        here = wet(lev * levels + l)
        wets = jnp.concatenate([low[4:6], here, high[4:6]], axis=0)
        speed = jnp.concatenate([low[1:2], zonal_ref[l], high[0:2]], axis=0)
        mixing = jnp.concatenate([low[3:4], lateral_ref[l], high[2:4]], axis=0)
        opened = wets[:-1] * wets[1:]
        opened_all[0, l] = opened[1 : columns + 1]
        spread_rows(zonal_fields, (l,), opened, speed, mixing, columns + 3)
        return carry

    def vert_build(row, carry):
        level = lev * levels + row - 1
        opened = wet(level - 1) * wet(level)
        spread_rows(
            vert_fields, (row,), opened, vert_ext[row + 1], vmix_ext[row + 1], columns
        )
        return carry

    def vert_opened(l, carry):
        level = lev * levels + l
        opened_all[2, l] = wet(level - 1) * wet(level)
        return carry

    def forward_zonal(g):
        def step(l, carry):
            def emit(x, value):
                middle[g, l + 2, x + 2] += value

            def keep(x, by_lower, by_upper):
                kept_zonal[0, g, l, x + 1] = by_lower
                kept_zonal[1, g, l, x + 1] = by_upper

            def keep_face(c, value):
                carried_all[0, g, l, c] = value

            forward_line(
                columns,
                lambda x: first[g, l + 2, x + 2],
                lambda c: zonal_fields[0, l, c + 1],
                lambda c: zonal_fields[1, l, c + 1],
                lambda c: zonal_fields[2, l, c + 1],
                emit,
                keep,
                keep_face,
            )
            return carry

        lax.fori_loop(0, levels, step, 0)

    def forward_vert(g):
        def step(i, carry):
            def emit(x, value):
                middle[g, x + 2, i + 2] += value

            def keep(x, by_lower, by_upper):
                kept_vert[0, g, x + 1, i] = by_lower
                kept_vert[1, g, x + 1, i] = by_upper

            def keep_face(c, value):
                carried_all[2, g, c, i] = value

            forward_line(
                levels,
                lambda x: first[g, x + 2, i + 2],
                lambda c: vert_fields[0, c + 1, i],
                lambda c: vert_fields[1, c + 1, i],
                lambda c: vert_fields[2, c + 1, i],
                emit,
                keep,
                keep_face,
            )
            return carry

        lax.fori_loop(0, columns, step, 0)

    def pull_merid(state, cot, store, g, fresh):
        def step(l, carry):
            for i in range(columns):
                own_cot = cot[g, l + 2, i + 2]
                pulled, share = backward_cell(
                    state[g, l + 2, i + 2],
                    own_cot,
                    merid_fields[0, l, i],
                    merid_fields[1, l, i],
                    merid_fields[2, l, i],
                    lane,
                    end,
                )
                store(g, l, i, own_cot + pulled, True)
                sums[1, l, i] = share if fresh else sums[1, l, i] + share
            return carry

        lax.fori_loop(0, levels, step, 0)

    def pull_zonal(state, cot, store, g, fresh):
        def step(l, carry):
            def speed(c, value):
                sums[0, l, c] = value if fresh else sums[0, l, c] + value

            backward_line(
                columns,
                lambda x: state[g, l + 2, x + 2],
                lambda x: cot[g, l + 2, x + 2],
                lambda c: zonal_fields[0, l, c + 1],
                lambda c: zonal_fields[1, l, c + 1],
                lambda c: zonal_fields[2, l, c + 1],
                lambda x, value: store(g, l, x, value, False),
                speed,
            )
            return carry

        lax.fori_loop(0, levels, step, 0)

    def pull_vert(state, cot, store, g, fresh):
        def step(i, carry):
            def speed(c, value):
                sums[2, c, i] = value if fresh else sums[2, c, i] + value

            backward_line(
                levels,
                lambda x: state[g, x + 2, i + 2],
                lambda x: cot[g, x + 2, i + 2],
                lambda c: vert_fields[0, c + 1, i],
                lambda c: vert_fields[1, c + 1, i],
                lambda c: vert_fields[2, c + 1, i],
                lambda x, value: store(g, x, i, value, False),
                speed,
            )
            return carry

        lax.fori_loop(0, columns, step, 0)

    def early_merid(g):
        def step(l, carry):
            for i in range(columns):
                own_cot = middle_cot[g, l + 2, i + 2]
                pulled, share = early_cell(
                    own_cot,
                    kept_merid[0, g, l, i],
                    kept_merid[1, g, l, i],
                    carried_all[1, g, l, i],
                    merid_fields[0, l, i],
                    merid_fields[1, l, i],
                    merid_fields[2, l, i],
                    lane,
                    end,
                )
                start_sum[g, l, i] = own_cot + pulled
                sums[1, l, i] += share
            return carry

        lax.fori_loop(0, levels, step, 0)

    def early_zonal(g, begin, count):
        def step(index, carry):
            l = lax.rem(begin + index, levels)

            def speed(c, value):
                sums[0, l, c] += value

            def emit(i, value):
                rows = pl.ds(g * ROWS * cells + l * columns + i, ROWS, stride=cells)
                start_ref[rows, :] = start_sum[g, l, i] + value

            early_line(
                columns,
                lambda x: middle_cot[g, l + 2, x + 2],
                lambda kind, x: kept_zonal[kind, g, l, x + 1],
                lambda c: carried_all[0, g, l, c],
                lambda c: zonal_fields[0, l, c + 1],
                lambda c: zonal_fields[1, l, c + 1],
                lambda c: zonal_fields[2, l, c + 1],
                emit,
                speed,
            )
            return carry

        lax.fori_loop(0, count, step, 0)

    def early_vert(g):
        def step(i, carry):
            def speed(c, value):
                sums[2, c, i] += value

            def emit(l, value):
                start_sum[g, l, i] += value

            early_line(
                levels,
                lambda x: middle_cot[g, x + 2, i + 2],
                lambda kind, x: kept_vert[kind, g, x + 1, i],
                lambda c: carried_all[2, g, c, i],
                lambda c: vert_fields[0, c + 1, i],
                lambda c: vert_fields[1, c + 1, i],
                lambda c: vert_fields[2, c + 1, i],
                emit,
                speed,
            )
            return carry

        lax.fori_loop(0, columns, step, 0)

    def store_middle(g, l, i, value, fresh):
        if fresh:
            middle_cot[g, l + 2, i + 2] = value
        else:
            middle_cot[g, l + 2, i + 2] += value

    for g in range(groups):
        arrive(first_copies[g], ("lev",))
        if g == 0:
            arrive(field_copies)
            lax.fori_loop(0, levels, zonal_build, 0)
            lax.fori_loop(0, levels + 3, vert_build, 0)
            lax.fori_loop(0, levels, vert_opened, 0)
        forward_vert(g)
        arrive(first_copies[g], ("tile",))
        forward_zonal(g)
        start(middle_copies[g])
    for g in range(groups):
        pull_merid(middle, last_cot, store_middle, g, g == 0)
    for g in range(groups):
        arrive(cot_copies[g])
        arrive(middle_copies[g], ("lev",))
        pull_vert(middle, last_cot, store_middle, g, g == 0)
        arrive(middle_copies[g], ("tile",))
        pull_zonal(middle, last_cot, store_middle, g, g == 0)
        start(back_copies[g])
    for g in range(groups):
        early_merid(g)
    for g in range(groups):
        arrive(back_copies[g], ("lev",))
        early_vert(g)

    share = levels // groups_trc
    sum_copies = []

    def reduce_rows(rows, begin, count):
        def step(index, carry):
            l = lax.rem(begin + index, levels)
            for row in rows:
                reduced[row, l] = opened_all[row, l] * jnp.sum(sums[row, l], axis=1)
            return carry

        lax.fori_loop(0, count, step, 0)

    def send_rows(part, rows):
        for step in range(1, groups_trc):
            target = lax.rem(trc + step, groups_trc)
            copy = pltpu.make_async_remote_copy(
                src_ref=reduced.at[rows, pl.ds(target * share, share)],
                dst_ref=arrived.at[step - 1, rows],
                send_sem=sum_send.at[part, step - 1],
                recv_sem=sum_recv.at[part, step - 1],
                device_id={"trc": target},
                device_id_type=MESH,
            )
            copy.start()
            sum_copies.append(copy)

    reduce_rows((1, 2), 0, levels)
    send_rows(0, pl.ds(1, 2))
    for g in range(groups):
        arrive(back_copies[g], ("tile",))
    after = (trc + 1) * share
    if groups_trc > 1:
        for g in range(groups):
            early_zonal(g, after, levels - share)
        reduce_rows((0,), after, levels - share)
        send_rows(1, pl.ds(0, 1))
    for g in range(groups):
        early_zonal(g, trc * share, share)
    reduce_rows((0,), trc * share, share)
    total = reduced[:, pl.ds(trc * share, share)]
    for copy in sum_copies:
        copy.wait_recv()
    for step in range(1, groups_trc):
        total = total + arrived[step - 1]
    speed_ref[...] = total

    for copies in [field_copies] + first_copies + cot_copies + middle_copies + back_copies:
        finish(copies)
    for copy in sum_copies:
        copy.wait_send()


def body(sizes, tracers, cotangent, *fields):
    count, levels, columns, lanes = tracers.shape
    groups = count // ROWS
    share = levels // sizes[2]
    extended = pltpu.VMEM((groups, levels + 4, columns + 4, ROWS, lanes), jnp.float32)
    flat = (count * levels * columns, lanes)
    start_cot, speed_cot = pl.pallas_call(
        functools.partial(kernel, sizes, tracers.shape),
        out_shape=(
            jax.ShapeDtypeStruct(flat, jnp.float32),
            jax.ShapeDtypeStruct((3, share, columns, lanes), jnp.float32),
        ),
        in_specs=[pl.BlockSpec(memory_space=pltpu.HBM)] * 8,
        out_specs=(pl.BlockSpec(memory_space=pltpu.VMEM),) * 2,
        scratch_shapes=[
            extended,
            extended,
            extended,
            extended,
            pltpu.VMEM((2, levels, 8, lanes), jnp.float32),
            pltpu.VMEM((2, levels, 8, lanes), jnp.float32),
            pltpu.VMEM((levels + 4, columns, lanes), jnp.float32),
            pltpu.VMEM((levels + 4, columns, lanes), jnp.float32),
            pltpu.VMEM((3, levels, columns + 3, ROWS, lanes), jnp.float32),
            pltpu.VMEM((3, levels + 3, columns, ROWS, lanes), jnp.float32),
            pltpu.VMEM((3, levels, columns, ROWS, lanes), jnp.float32),
            pltpu.VMEM((3, levels, columns, lanes), jnp.float32),
            pltpu.VMEM((3, levels, columns, ROWS, lanes), jnp.float32),
            pltpu.VMEM((3, levels, columns, lanes), jnp.float32),
            pltpu.VMEM((max(sizes[2] - 1, 1), 3, share, columns, lanes), jnp.float32),
            pltpu.SemaphoreType.DMA((4, groups, 4)),
            pltpu.SemaphoreType.DMA((4, groups, 4)),
            pltpu.SemaphoreType.DMA((2, 4)),
            pltpu.SemaphoreType.DMA((2, 4)),
            pltpu.SemaphoreType.DMA((2, max(sizes[2] - 1, 1))),
            pltpu.SemaphoreType.DMA((2, max(sizes[2] - 1, 1))),
            pltpu.VMEM((groups, levels, columns, ROWS, lanes), jnp.float32),
            pltpu.VMEM((2, groups, levels, columns + 2, ROWS, lanes), jnp.float32),
            pltpu.VMEM((2, groups, levels + 2, columns, ROWS, lanes), jnp.float32),
            pltpu.VMEM((2, groups, levels, columns, ROWS, lanes), jnp.float32),
            pltpu.VMEM((3, groups, levels, columns, ROWS, lanes), jnp.float32),
            pltpu.SemaphoreType.DMA((8,)),
            pltpu.VMEM(flat, jnp.float32),
            pltpu.VMEM(flat, jnp.float32),
            *[pltpu.VMEM(values.shape, values.dtype) for values in fields],
        ],
        compiler_params=pltpu.CompilerParams(
            collective_id=0, has_side_effects=True, vmem_limit_bytes=60 * 1024 * 1024
        ),
    )(tracers.reshape(flat), cotangent.reshape(flat), *fields)
    return start_cot.reshape(tracers.shape), speed_cot


def solution(mesh):
    sizes = (mesh.shape["tile"], mesh.shape["lev"], mesh.shape["trc"])
    return jax.shard_map(
        functools.partial(body, sizes),
        mesh=mesh,
        in_specs=(
            P("trc", "lev", ("ens", "tile"), None),
            P("trc", "lev", ("ens", "tile"), None),
            P("lev", ("ens", "tile"), None),
            P("lev", ("ens", "tile"), None),
            P("lev", ("ens", "tile"), None),
            P("lev", ("ens", "tile"), None),
            P("lev", ("ens", "tile"), None),
            P(("ens", "tile"), None),
        ),
        out_specs=(
            P("trc", "lev", ("ens", "tile"), None),
            P(None, ("lev", "trc"), ("ens", "tile"), None),
        ),
        check_vma=False,
    )
```

```python
import functools

import jax
import jax.numpy as jnp
from jax import lax
from jax.experimental import pallas as pl
from jax.experimental.pallas import tpu as pltpu
from jax.sharding import PartitionSpec as P

ALBADA_FLOOR = 0.01
MESH = pl.DeviceIdType.MESH
ROWS = 8


def inverse(values):
    return pl.reciprocal(values, approx=True)


def limiter(lower, upper, lower_square, upper_square):
    half_inverse = inverse(lower_square + upper_square)
    product = lower * upper
    total = lower + upper
    return product * total * half_inverse, half_inverse, total


def doubled_square(step):
    return step * (step + step) + ALBADA_FLOOR


def slopes(lower, upper, slope, half_inverse, total):
    fourfold = 4.0 * slope
    by_lower = (upper * (lower + total) - lower * fourfold) * half_inverse
    by_upper = (lower * (upper + total) - upper * fourfold) * half_inverse
    return by_lower, by_upper


def forward_line(count, q, rise, fall, spread, emit, keep, keep_face):
    values = {x: q(x) for x in range(-2, count + 2)}
    steps = {c: values[c] - values[c - 1] for c in range(-1, count + 2)}
    squares = {c: doubled_square(steps[c]) for c in steps}
    through = {}
    above = None
    for x in range(-1, count + 1):
        parts = limiter(steps[x], steps[x + 1], squares[x], squares[x + 1])
        slope = parts[0]
        keep(x, *slopes(steps[x], steps[x + 1], *parts))
        if x >= 0:
            falls = fall(x)
            carried = jnp.where(falls < 0.0, values[x] - slope, above)
            through[x] = (rise(x) + falls) * carried - spread(x) * steps[x]
            if x < count:
                keep_face(x, carried)
        above = values[x] + slope
        if x >= 1:
            emit(x - 1, through[x - 1] - through[x])


def backward_line(count, q, g, rise, fall, spread, emit, speed):
    values = {x: q(x) for x in range(-2, count + 2)}
    steps = {c: values[c] - values[c - 1] for c in range(-1, count + 2)}
    squares = {c: doubled_square(steps[c]) for c in steps}
    cots = {x: g(x) for x in range(-2, count + 2)}
    up, down, jump, falls = {}, {}, {}, {}
    faces = {c: cots[c] - cots[c - 1] for c in range(-1, count + 2)}
    for c in range(0, count + 2):
        up[c] = faces[c] * rise(c)
    for c in range(-1, count + 1):
        falls[c] = fall(c)
        down[c] = faces[c] * falls[c]
    above, later = None, None
    for x in range(-1, count + 1):
        lower, upper = steps[x], steps[x + 1]
        slope, half_inverse, total = limiter(lower, upper, squares[x], squares[x + 1])
        weight = half_inverse * (up[x + 1] - down[x])
        fourfold = 4.0 * slope
        if x >= 0:
            first = (upper * (lower + total) - lower * fourfold) * weight
            jump[x] = first + later - spread(x) * faces[x]
        if x < count:
            later = (lower * (upper + total) - upper * fourfold) * weight
        if 0 <= x < count:
            carried = jnp.where(falls[x] < 0.0, values[x] - slope, above)
            speed(x, faces[x] * carried)
        above = values[x] + slope
        if x >= 1:
            emit(x - 1, (jump[x - 1] - jump[x]) + (up[x] + down[x - 1]))


def early_line(count, g, kept, carried, rise, fall, spread, emit, speed):
    cots = {x: g(x) for x in range(-2, count + 2)}
    faces = {c: cots[c] - cots[c - 1] for c in range(-1, count + 2)}
    up = {c: faces[c] * rise(c) for c in range(0, count + 2)}
    down = {c: faces[c] * fall(c) for c in range(-1, count + 1)}
    jump, later = {}, None
    for x in range(-1, count + 1):
        weight = up[x + 1] - down[x]
        if x >= 0:
            jump[x] = kept(0, x) * weight + later - spread(x) * faces[x]
        if x < count:
            later = kept(1, x) * weight
        if 0 <= x < count:
            speed(x, faces[x] * carried(x))
        if x >= 1:
            emit(x - 1, (jump[x - 1] - jump[x]) + (up[x] + down[x - 1]))


def across(values, lane, last):
    before = jnp.where(lane == 0, 0.0, pltpu.roll(values, 1, 1))
    lower = values - before
    upper = jnp.where(lane == last, -values, pltpu.roll(lower, last, 1))
    return lower, upper


def forward_cell(values, rise, fall, spread, lane, last):
    lower, upper = across(values, lane, last)
    parts = limiter(lower, upper, doubled_square(lower), doubled_square(upper))
    slope = parts[0]
    above = pltpu.roll(values + slope, 1, 1)
    carried = jnp.where(fall < 0.0, values - slope, above)
    through = (rise + fall) * carried - spread * lower
    kept = slopes(lower, upper, *parts)
    return through - pltpu.roll(through, last, 1), kept, carried


def backward_cell(values, cot, rise, fall, spread, lane, last):
    lower, upper = across(values, lane, last)
    slope, half_inverse, total = limiter(
        lower, upper, doubled_square(lower), doubled_square(upper)
    )
    face = cot - pltpu.roll(cot, 1, 1)
    up = pltpu.roll(face * rise, last, 1)
    down = face * fall
    weight = half_inverse * (up - down)
    fourfold = 4.0 * slope
    first = (upper * (lower + total) - lower * fourfold) * weight
    later = (lower * (upper + total) - upper * fourfold) * weight
    near = first - spread * face
    result = (
        near
        - later
        + up
        + down
        + jnp.where(lane == 0, 0.0, pltpu.roll(later, 1, 1))
        - jnp.where(lane == last, 0.0, pltpu.roll(near, last, 1))
    )
    carried = jnp.where(fall < 0.0, values - slope, pltpu.roll(values + slope, 1, 1))
    return result, face * carried


def early_cell(cot, by_lower, by_upper, carried, rise, fall, spread, lane, last):
    face = cot - pltpu.roll(cot, 1, 1)
    up = pltpu.roll(face * rise, last, 1)
    down = face * fall
    weight = up - down
    later = by_upper * weight
    near = by_lower * weight - spread * face
    result = (
        near
        - later
        + up
        + down
        + jnp.where(lane == 0, 0.0, pltpu.roll(later, 1, 1))
        - jnp.where(lane == last, 0.0, pltpu.roll(near, last, 1))
    )
    return result, face * carried


def kernel(
    sizes,
    dims,
    tracer_hbm,
    cot_hbm,
    zonal_hbm,
    merid_hbm,
    vert_hbm,
    lateral_hbm,
    vmix_hbm,
    depth_hbm,
    start_ref,
    speed_ref,
    first,
    last_cot,
    middle,
    middle_cot,
    pack,
    packed,
    vert_ext,
    vmix_ext,
    zonal_fields,
    vert_fields,
    merid_fields,
    opened_all,
    sums,
    reduced,
    arrived,
    halo_send,
    halo_recv,
    field_send,
    field_recv,
    sum_send,
    sum_recv,
    start_sum,
    kept_zonal,
    kept_vert,
    kept_merid,
    carried_all,
    load_sem,
    *loaded,
):
    outside = (
        tracer_hbm,
        cot_hbm,
        zonal_hbm,
        merid_hbm,
        vert_hbm,
        lateral_hbm,
        vmix_hbm,
        depth_hbm,
    )
    loads = [
        pltpu.make_async_copy(source, target, load_sem.at[row])
        for row, (source, target) in enumerate(zip(outside, loaded))
    ]
    for load in loads:
        load.start()
    (
        tracer_ref,
        cot_ref,
        zonal_ref,
        merid_ref,
        vert_ref,
        lateral_ref,
        vmix_ref,
        depth_ref,
    ) = loaded
    tiles, levs, groups_trc = sizes
    tracers, levels, columns, lanes = dims
    groups = tracers // ROWS
    end = lanes - 1
    cells = levels * columns
    tile, lev, trc = lax.axis_index("tile"), lax.axis_index("lev"), lax.axis_index("trc")
    lane = lax.broadcasted_iota(jnp.int32, (ROWS, lanes), 1)

    below = {"tile": tile > 0, "lev": lev > 0}
    beyond = {"tile": tile < tiles - 1, "lev": lev < levs - 1}
    place = {"tile": tile, "lev": lev}
    size = {"tile": tiles, "lev": levs}
    axes = [axis for axis in ("tile", "lev") if size[axis] > 1]

    barrier = pltpu.get_barrier_semaphore()
    expected = groups_trc - 1
    for axis in axes:
        for there, offset in ((below[axis], -1), (beyond[axis], 1)):

            @pl.when(there)
            def _(axis=axis, offset=offset):
                pl.semaphore_signal(
                    barrier,
                    inc=1,
                    device_id={axis: place[axis] + offset},
                    device_id_type=MESH,
                )

            expected = expected + there.astype(jnp.int32)
    for step in range(1, groups_trc):
        pl.semaphore_signal(
            barrier,
            inc=1,
            device_id={"trc": lax.rem(trc + step, groups_trc)},
            device_id_type=MESH,
        )

    def wet(level):
        known = jnp.logical_and(level < depth_ref[...], level >= 0)
        return jnp.where(known, 1.0, 0.0)

    def load_own(l, carry):
        for g in range(groups):
            for i in range(columns):
                rows = pl.ds(g * ROWS * cells + l * columns + i, ROWS, stride=cells)
                first[g, l + 2, i + 2] = tracer_ref[rows, :]
                last_cot[g, l + 2, i + 2] = cot_ref[rows, :]
        here = wet(lev * levels + l)
        zonal, lateral = zonal_ref[l], lateral_ref[l]
        for side, rows in ((0, slice(0, 2)), (1, slice(columns - 2, columns))):
            pack[side, l] = jnp.concatenate(
                [zonal[rows], lateral[rows], here[rows], here[rows]], axis=0
            )
        vert_ext[l + 2] = vert_ref[l]
        vmix_ext[l + 2] = vmix_ref[l]
        return carry

    zero_tile = jnp.zeros((ROWS, lanes), jnp.float32)

    def clear(side):
        for buffer in (first, last_cot, middle, middle_cot):
            for g in range(groups):
                if side < 2:
                    place_at = columns + 2 if side == 0 else 0

                    def clear_row(l, carry):
                        buffer[g, l + 2, place_at] = zero_tile
                        buffer[g, l + 2, place_at + 1] = zero_tile
                        return carry

                    lax.fori_loop(0, levels, clear_row, 0)
                else:
                    place_at = levels + 2 if side == 2 else 0

                    def clear_column(i, carry):
                        buffer[g, place_at, i + 2] = zero_tile
                        buffer[g, place_at + 1, i + 2] = zero_tile
                        return carry

                    lax.fori_loop(0, columns, clear_column, 0)
        if side < 2:
            packed[side] = jnp.zeros_like(packed[side])
        else:
            place_at = levels + 2 if side == 2 else 0
            for buffer in (vert_ext, vmix_ext):
                buffer[place_at] = zero_tile_rows
                buffer[place_at + 1] = zero_tile_rows

    zero_tile_rows = jnp.zeros((columns, lanes), jnp.float32)
    for side, axis, there in (
        (0, "tile", beyond["tile"]),
        (1, "tile", below["tile"]),
        (2, "lev", beyond["lev"]),
        (3, "lev", below["lev"]),
    ):
        if size[axis] > 1:

            @pl.when(jnp.logical_not(there))
            def _(side=side):
                clear(side)

        else:
            clear(side)

    for load in loads:
        load.wait()
    lax.fori_loop(0, levels, load_own, 0)

    pl.semaphore_wait(barrier, expected)

    def exchange(pairs, send_sem, recv_sem):
        copies = []
        for side, source, destination in pairs:
            axis = "tile" if side in (0, 1) else "lev"
            if size[axis] == 1:
                continue
            goes_down = side in (0, 2)
            copy = pltpu.make_async_remote_copy(
                src_ref=source,
                dst_ref=destination,
                send_sem=send_sem(side),
                recv_sem=recv_sem(side),
                device_id={axis: place[axis] + (-1 if goes_down else 1)},
                device_id_type=MESH,
            )
            sends = below[axis] if goes_down else beyond[axis]
            receives = beyond[axis] if goes_down else below[axis]
            copies.append((copy, sends, receives, axis))
        return copies

    def start(copies):
        for copy, sends, _, _ in copies:
            pl.when(sends)(copy.start)

    def arrive(copies, along=("tile", "lev")):
        for copy, _, receives, axis in copies:
            if axis in along:
                pl.when(receives)(copy.wait_recv)

    def finish(copies):
        for copy, sends, _, _ in copies:
            pl.when(sends)(copy.wait_send)

    own_l, own_i = pl.ds(2, levels), pl.ds(2, columns)

    def halo(buffer, stage, g):
        pairs = [
            (0, buffer.at[g, own_l, pl.ds(2, 2)], buffer.at[g, own_l, pl.ds(columns + 2, 2)]),
            (1, buffer.at[g, own_l, pl.ds(columns, 2)], buffer.at[g, own_l, pl.ds(0, 2)]),
            (2, buffer.at[g, pl.ds(2, 2), own_i], buffer.at[g, pl.ds(levels + 2, 2), own_i]),
            (3, buffer.at[g, pl.ds(levels, 2), own_i], buffer.at[g, pl.ds(0, 2), own_i]),
        ]
        return exchange(
            pairs,
            lambda side: halo_send.at[stage, g, side],
            lambda side: halo_recv.at[stage, g, side],
        )

    field_copies = exchange(
        [(0, pack.at[0], packed.at[0]), (1, pack.at[1], packed.at[1])],
        lambda side: field_send.at[0, side],
        lambda side: field_recv.at[0, side],
    )
    for row, buffer in enumerate((vert_ext, vmix_ext)):
        field_copies += exchange(
            [
                (2, buffer.at[pl.ds(2, 2)], buffer.at[pl.ds(levels + 2, 2)]),
                (3, buffer.at[pl.ds(levels, 2)], buffer.at[pl.ds(0, 2)]),
            ],
            lambda side, row=row: field_send.at[row, side],
            lambda side, row=row: field_recv.at[row, side],
        )
    first_copies = [halo(first, 0, g) for g in range(groups)]
    cot_copies = [halo(last_cot, 1, g) for g in range(groups)]
    middle_copies = [halo(middle, 2, g) for g in range(groups)]
    back_copies = [halo(middle_cot, 3, g) for g in range(groups)]

    start(first_copies[0])
    start(field_copies)
    for copies in first_copies[1:] + cot_copies:
        start(copies)

    def spread_rows(target, head, opened, speed, mixing, count):
        kinds = (
            opened * jnp.maximum(speed, 0.0),
            opened * jnp.minimum(speed, 0.0),
            opened * mixing,
        )
        for kind, values in enumerate(kinds):
            for i in range(count):
                target[(kind,) + head + (i,)] = jnp.broadcast_to(
                    values[i : i + 1], (ROWS, lanes)
                )

    def merid_build(l, carry):
        here = wet(lev * levels + l)
        south = jnp.where(lane[:columns] == 0, 0.0, pltpu.roll(here, 1, 1))
        opened = here * south
        opened_all[1, l] = opened
        spread_rows(merid_fields, (l,), opened, merid_ref[l], lateral_ref[l], columns)
        return carry

    lax.fori_loop(0, levels, merid_build, 0)

    def forward_merid(g):
        def step(l, carry):
            for i in range(columns):
                values = first[g, l + 2, i + 2]
                gain, kept, carried = forward_cell(
                    values,
                    merid_fields[0, l, i],
                    merid_fields[1, l, i],
                    merid_fields[2, l, i],
                    lane,
                    end,
                )
                middle[g, l + 2, i + 2] = values + gain
                kept_merid[0, g, l, i] = kept[0]
                kept_merid[1, g, l, i] = kept[1]
                carried_all[1, g, l, i] = carried
            return carry

        lax.fori_loop(0, levels, step, 0, unroll=2)

    for g in range(groups):
        forward_merid(g)

    def zonal_build(l, carry):
        low, high = packed[1, l], packed[0, l]
        here = wet(lev * levels + l)
        wets = jnp.concatenate([low[4:6], here, high[4:6]], axis=0)
        speed = jnp.concatenate([low[1:2], zonal_ref[l], high[0:2]], axis=0)
        mixing = jnp.concatenate([low[3:4], lateral_ref[l], high[2:4]], axis=0)
        opened = wets[:-1] * wets[1:]
        opened_all[0, l] = opened[1 : columns + 1]
        spread_rows(zonal_fields, (l,), opened, speed, mixing, columns + 3)
        return carry

    def vert_build(row, carry):
        level = lev * levels + row - 1
        opened = wet(level - 1) * wet(level)
        spread_rows(
            vert_fields, (row,), opened, vert_ext[row + 1], vmix_ext[row + 1], columns
        )
        return carry

    def vert_opened(l, carry):
        level = lev * levels + l
        opened_all[2, l] = wet(level - 1) * wet(level)
        return carry

    def forward_zonal(g):
        def step(l, carry):
            def emit(x, value):
                middle[g, l + 2, x + 2] += value

            def keep(x, by_lower, by_upper):
                kept_zonal[0, g, l, x + 1] = by_lower
                kept_zonal[1, g, l, x + 1] = by_upper

            def keep_face(c, value):
                carried_all[0, g, l, c] = value

            forward_line(
                columns,
                lambda x: first[g, l + 2, x + 2],
                lambda c: zonal_fields[0, l, c + 1],
                lambda c: zonal_fields[1, l, c + 1],
                lambda c: zonal_fields[2, l, c + 1],
                emit,
                keep,
                keep_face,
            )
            return carry

        lax.fori_loop(0, levels, step, 0, unroll=2)

    def forward_vert(g):
        def step(i, carry):
            def emit(x, value):
                middle[g, x + 2, i + 2] += value

            def keep(x, by_lower, by_upper):
                kept_vert[0, g, x + 1, i] = by_lower
                kept_vert[1, g, x + 1, i] = by_upper

            def keep_face(c, value):
                carried_all[2, g, c, i] = value

            forward_line(
                levels,
                lambda x: first[g, x + 2, i + 2],
                lambda c: vert_fields[0, c + 1, i],
                lambda c: vert_fields[1, c + 1, i],
                lambda c: vert_fields[2, c + 1, i],
                emit,
                keep,
                keep_face,
            )
            return carry

        lax.fori_loop(0, columns, step, 0, unroll=2)

    def pull_merid(state, cot, store, g, fresh):
        def step(l, carry):
            for i in range(columns):
                own_cot = cot[g, l + 2, i + 2]
                pulled, share = backward_cell(
                    state[g, l + 2, i + 2],
                    own_cot,
                    merid_fields[0, l, i],
                    merid_fields[1, l, i],
                    merid_fields[2, l, i],
                    lane,
                    end,
                )
                store(g, l, i, own_cot + pulled, True)
                sums[1, l, i] = share if fresh else sums[1, l, i] + share
            return carry

        lax.fori_loop(0, levels, step, 0, unroll=2)

    def pull_zonal(state, cot, store, g, fresh):
        def step(l, carry):
            def speed(c, value):
                sums[0, l, c] = value if fresh else sums[0, l, c] + value

            backward_line(
                columns,
                lambda x: state[g, l + 2, x + 2],
                lambda x: cot[g, l + 2, x + 2],
                lambda c: zonal_fields[0, l, c + 1],
                lambda c: zonal_fields[1, l, c + 1],
                lambda c: zonal_fields[2, l, c + 1],
                lambda x, value: store(g, l, x, value, False),
                speed,
            )
            return carry

        lax.fori_loop(0, levels, step, 0, unroll=2)

    def pull_vert(state, cot, store, g, fresh):
        def step(i, carry):
            def speed(c, value):
                sums[2, c, i] = value if fresh else sums[2, c, i] + value

            backward_line(
                levels,
                lambda x: state[g, x + 2, i + 2],
                lambda x: cot[g, x + 2, i + 2],
                lambda c: vert_fields[0, c + 1, i],
                lambda c: vert_fields[1, c + 1, i],
                lambda c: vert_fields[2, c + 1, i],
                lambda x, value: store(g, x, i, value, False),
                speed,
            )
            return carry

        lax.fori_loop(0, columns, step, 0, unroll=2)

    def early_merid(g):
        def step(l, carry):
            for i in range(columns):
                own_cot = middle_cot[g, l + 2, i + 2]
                pulled, share = early_cell(
                    own_cot,
                    kept_merid[0, g, l, i],
                    kept_merid[1, g, l, i],
                    carried_all[1, g, l, i],
                    merid_fields[0, l, i],
                    merid_fields[1, l, i],
                    merid_fields[2, l, i],
                    lane,
                    end,
                )
                start_sum[g, l, i] = own_cot + pulled
                sums[1, l, i] += share
            return carry

        lax.fori_loop(0, levels, step, 0, unroll=2)

    def early_zonal(g, begin, count):
        def step(index, carry):
            l = lax.rem(begin + index, levels)

            def speed(c, value):
                sums[0, l, c] += value

            def emit(i, value):
                rows = pl.ds(g * ROWS * cells + l * columns + i, ROWS, stride=cells)
                start_ref[rows, :] = start_sum[g, l, i] + value

            early_line(
                columns,
                lambda x: middle_cot[g, l + 2, x + 2],
                lambda kind, x: kept_zonal[kind, g, l, x + 1],
                lambda c: carried_all[0, g, l, c],
                lambda c: zonal_fields[0, l, c + 1],
                lambda c: zonal_fields[1, l, c + 1],
                lambda c: zonal_fields[2, l, c + 1],
                emit,
                speed,
            )
            return carry

        lax.fori_loop(0, count, step, 0, unroll=2)

    def early_vert(g):
        def step(i, carry):
            def speed(c, value):
                sums[2, c, i] += value

            def emit(l, value):
                start_sum[g, l, i] += value

            early_line(
                levels,
                lambda x: middle_cot[g, x + 2, i + 2],
                lambda kind, x: kept_vert[kind, g, x + 1, i],
                lambda c: carried_all[2, g, c, i],
                lambda c: vert_fields[0, c + 1, i],
                lambda c: vert_fields[1, c + 1, i],
                lambda c: vert_fields[2, c + 1, i],
                emit,
                speed,
            )
            return carry

        lax.fori_loop(0, columns, step, 0, unroll=2)

    def store_middle(g, l, i, value, fresh):
        if fresh:
            middle_cot[g, l + 2, i + 2] = value
        else:
            middle_cot[g, l + 2, i + 2] += value

    for g in range(groups):
        arrive(first_copies[g], ("lev",))
        if g == 0:
            arrive(field_copies)
            lax.fori_loop(0, levels, zonal_build, 0)
            lax.fori_loop(0, levels + 3, vert_build, 0)
            lax.fori_loop(0, levels, vert_opened, 0)
        forward_vert(g)
        arrive(first_copies[g], ("tile",))
        forward_zonal(g)
        start(middle_copies[g])
    for g in range(groups):
        pull_merid(middle, last_cot, store_middle, g, g == 0)
    for g in range(groups):
        arrive(cot_copies[g])
        arrive(middle_copies[g], ("lev",))
        pull_vert(middle, last_cot, store_middle, g, g == 0)
        arrive(middle_copies[g], ("tile",))
        pull_zonal(middle, last_cot, store_middle, g, g == 0)
        start(back_copies[g])
    for g in range(groups):
        early_merid(g)
    for g in range(groups):
        arrive(back_copies[g], ("lev",))
        early_vert(g)

    share = levels // groups_trc
    sum_copies = []

    def reduce_rows(rows, begin, count):
        def step(index, carry):
            l = lax.rem(begin + index, levels)
            for row in rows:
                reduced[row, l] = opened_all[row, l] * jnp.sum(sums[row, l], axis=1)
            return carry

        lax.fori_loop(0, count, step, 0, unroll=2)

    def send_rows(part, rows):
        for step in range(1, groups_trc):
            target = lax.rem(trc + step, groups_trc)
            copy = pltpu.make_async_remote_copy(
                src_ref=reduced.at[rows, pl.ds(target * share, share)],
                dst_ref=arrived.at[step - 1, rows],
                send_sem=sum_send.at[part, step - 1],
                recv_sem=sum_recv.at[part, step - 1],
                device_id={"trc": target},
                device_id_type=MESH,
            )
            copy.start()
            sum_copies.append(copy)

    reduce_rows((1, 2), 0, levels)
    send_rows(0, pl.ds(1, 2))
    for g in range(groups):
        arrive(back_copies[g], ("tile",))
    after = (trc + 1) * share
    if groups_trc > 1:
        for g in range(groups):
            early_zonal(g, after, levels - share)
        reduce_rows((0,), after, levels - share)
        send_rows(1, pl.ds(0, 1))
    for g in range(groups):
        early_zonal(g, trc * share, share)
    reduce_rows((0,), trc * share, share)
    total = reduced[:, pl.ds(trc * share, share)]
    for copy in sum_copies:
        copy.wait_recv()
    for step in range(1, groups_trc):
        total = total + arrived[step - 1]
    speed_ref[...] = total

    for copies in [field_copies] + first_copies + cot_copies + middle_copies + back_copies:
        finish(copies)
    for copy in sum_copies:
        copy.wait_send()


def body(sizes, tracers, cotangent, *fields):
    count, levels, columns, lanes = tracers.shape
    groups = count // ROWS
    share = levels // sizes[2]
    extended = pltpu.VMEM((groups, levels + 4, columns + 4, ROWS, lanes), jnp.float32)
    flat = (count * levels * columns, lanes)
    start_cot, speed_cot = pl.pallas_call(
        functools.partial(kernel, sizes, tracers.shape),
        out_shape=(
            jax.ShapeDtypeStruct(flat, jnp.float32),
            jax.ShapeDtypeStruct((3, share, columns, lanes), jnp.float32),
        ),
        in_specs=[pl.BlockSpec(memory_space=pltpu.HBM)] * 8,
        out_specs=(pl.BlockSpec(memory_space=pltpu.VMEM),) * 2,
        scratch_shapes=[
            extended,
            extended,
            extended,
            extended,
            pltpu.VMEM((2, levels, 8, lanes), jnp.float32),
            pltpu.VMEM((2, levels, 8, lanes), jnp.float32),
            pltpu.VMEM((levels + 4, columns, lanes), jnp.float32),
            pltpu.VMEM((levels + 4, columns, lanes), jnp.float32),
            pltpu.VMEM((3, levels, columns + 3, ROWS, lanes), jnp.float32),
            pltpu.VMEM((3, levels + 3, columns, ROWS, lanes), jnp.float32),
            pltpu.VMEM((3, levels, columns, ROWS, lanes), jnp.float32),
            pltpu.VMEM((3, levels, columns, lanes), jnp.float32),
            pltpu.VMEM((3, levels, columns, ROWS, lanes), jnp.float32),
            pltpu.VMEM((3, levels, columns, lanes), jnp.float32),
            pltpu.VMEM((max(sizes[2] - 1, 1), 3, share, columns, lanes), jnp.float32),
            pltpu.SemaphoreType.DMA((4, groups, 4)),
            pltpu.SemaphoreType.DMA((4, groups, 4)),
            pltpu.SemaphoreType.DMA((2, 4)),
            pltpu.SemaphoreType.DMA((2, 4)),
            pltpu.SemaphoreType.DMA((2, max(sizes[2] - 1, 1))),
            pltpu.SemaphoreType.DMA((2, max(sizes[2] - 1, 1))),
            pltpu.VMEM((groups, levels, columns, ROWS, lanes), jnp.float32),
            pltpu.VMEM((2, groups, levels, columns + 2, ROWS, lanes), jnp.float32),
            pltpu.VMEM((2, groups, levels + 2, columns, ROWS, lanes), jnp.float32),
            pltpu.VMEM((2, groups, levels, columns, ROWS, lanes), jnp.float32),
            pltpu.VMEM((3, groups, levels, columns, ROWS, lanes), jnp.float32),
            pltpu.SemaphoreType.DMA((8,)),
            pltpu.VMEM(flat, jnp.float32),
            pltpu.VMEM(flat, jnp.float32),
            *[pltpu.VMEM(values.shape, values.dtype) for values in fields],
        ],
        compiler_params=pltpu.CompilerParams(
            collective_id=0, has_side_effects=True, vmem_limit_bytes=60 * 1024 * 1024
        ),
    )(tracers.reshape(flat), cotangent.reshape(flat), *fields)
    return start_cot.reshape(tracers.shape), speed_cot


def solution(mesh):
    sizes = (mesh.shape["tile"], mesh.shape["lev"], mesh.shape["trc"])
    return jax.shard_map(
        functools.partial(body, sizes),
        mesh=mesh,
        in_specs=(
            P("trc", "lev", ("ens", "tile"), None),
            P("trc", "lev", ("ens", "tile"), None),
            P("lev", ("ens", "tile"), None),
            P("lev", ("ens", "tile"), None),
            P("lev", ("ens", "tile"), None),
            P("lev", ("ens", "tile"), None),
            P("lev", ("ens", "tile"), None),
            P(("ens", "tile"), None),
        ),
        out_specs=(
            P("trc", "lev", ("ens", "tile"), None),
            P(None, ("lev", "trc"), ("ens", "tile"), None),
        ),
        check_vma=False,
    )
```
